256 devices in a mesh: dp: 16 (over z_hi, x, core), cell: 16 (over z_lo, y).
Axes of the slice: x: 4, y: 4, z: 8 (z_hi: 2, z_lo: 4; z = z_hi * 4 + z_lo), core: 2. Of those that a mesh axis runs over, the one named last changes fastest.
Arguments:
- jacobian: float32 [1024, 64, 64, 32], P('dp', 'cell'), may hold values from -0.03314563 to 0.03314563
- smooth_x: float32 [4, 64, 64], replicated, may hold values from 0 to 1.5, as said below
- smooth_y: float32 [4, 64, 64], replicated, may hold values from 0 to 1.5, as said below
- smooth_z: float32 [4, 32, 32], replicated, may hold values from 0 to 1.5, as said below
- index_x: int32 [64, 32], replicated, may hold values from 0 to 3
- index_y: int32 [64, 32], P('cell'), may hold values from 0 to 3
- index_z: int32 [64, 64], P('cell'), may hold values from 0 to 3
Outputs:
- normal_matrix: float32 [1024, 1024], P('dp', 'cell')
The draws below stay inside these ranges and needn't reach their ends.
Inputs may be any that keep to these rules, and one draw needn't show every extreme that they name: `smooth_x`: zero where the two indices differ by more than 3; nonnegative. `smooth_y`: zero where the two indices differ by more than 3; nonnegative. `smooth_z`: zero where the two indices differ by more than 3; nonnegative.
All inputs are finite; a program needn't handle non-finite values.
Results may differ from the reference program's by a relative error of at most 0.003.
Values may be sent and summed in bfloat16 or wider, within the bound.
No kernel may reach another device: no remote copies, remote signals or barrier semaphores. Data moves between devices by JAX's collectives and lax.ppermute only.
A program may use at most 64 MiB of HBM per device.

```python
import jax
import jax.numpy as jnp
from jax import lax

NX = 64
NY = 64
NZ = 32
KLEN = 4
BAND = 3
M = 1024


def banded_table(key, count):
    first_key, second_key = jax.random.split(key)
    places = jnp.arange(count)
    distance = jnp.abs(places[:, None] - places[None, :])
    diagonal = jax.random.uniform(first_key, (KLEN, count, count), jnp.float32, 1.0, 1.5)
    offside = jax.random.uniform(second_key, (KLEN, count, count), jnp.float32, 0.05, 0.15)
    return jnp.where(distance == 0, diagonal, jnp.where(distance <= BAND, offside, jnp.float32(0.0)))


def draw_smooth_x(key, part):
    key = jax.random.fold_in(key, 11)
    return banded_table(key, NX)


def draw_smooth_y(key, part):
    key = jax.random.fold_in(key, 12)
    return banded_table(key, NY)


def draw_smooth_z(key, part):
    key = jax.random.fold_in(key, 13)
    return banded_table(key, NZ)


def draw_jacobian(key, part):
    key = jax.random.fold_in(key, 14)
    keys = jax.random.split(key, 3)
    scale = 1.0 / (NX * NY * NZ) ** 0.5
    noise = jax.random.truncated_normal(keys[0], -4.0, 4.0, (M, NX, NY, NZ), jnp.float32)
    common = jax.random.truncated_normal(keys[1], -4.0, 4.0, (1, NX, NY, NZ), jnp.float32)
    weights = jax.random.truncated_normal(keys[2], -4.0, 4.0, (M, 1, 1, 1), jnp.float32)
    return ((0.5 * weights * common + noise) * scale).astype(jnp.float32)


def touch_ends(values, rng, least, high):
    extent = values.shape
    index_at = [jax.random.randint(jax.random.fold_in(rng, axis), (), 0, extent[axis]) for axis in range(len(extent))]
    values = values.at[tuple(index_at)].set(least)
    longest = extent.index(max(extent))
    index_at[longest] = (index_at[longest] + 1) % extent[longest]
    return values.at[tuple(index_at)].set(high)


def setup_inputs(seed: int = 0) -> dict:
    seeds = jax.random.split(jax.random.key(seed), 8)
    return {
        "jacobian": draw_jacobian(jax.random.fold_in(seeds[7], 71), 0),
        "smooth_x": draw_smooth_x(jax.random.fold_in(seeds[7], 71), 0),
        "smooth_y": draw_smooth_y(jax.random.fold_in(seeds[7], 71), 0),
        "smooth_z": draw_smooth_z(jax.random.fold_in(seeds[7], 71), 0),
        "index_x": touch_ends(jax.random.randint(seeds[4], (NY, NZ), 0, KLEN), jax.random.fold_in(seeds[4], 1), 0, KLEN - 1).astype(jnp.int32),
        "index_y": touch_ends(jax.random.randint(seeds[5], (NX, NZ), 0, KLEN), jax.random.fold_in(seeds[5], 1), 0, KLEN - 1).astype(jnp.int32),
        "index_z": touch_ends(jax.random.randint(seeds[6], (NX, NY), 0, KLEN), jax.random.fold_in(seeds[6], 1), 0, KLEN - 1).astype(jnp.int32),
    }


def select_apply(tables, labels, operand, form, target):
    running = jnp.zeros(operand.shape, jnp.float32)
    for table_no in range(tables.shape[0]):
        smoothed = jnp.einsum(form, tables[table_no], operand, precision=lax.Precision.HIGHEST)
        running = running + jnp.where(labels.reshape(target) == table_no, smoothed, jnp.float32(0.0))
    return running


def reference(jacobian, smooth_x, smooth_y, smooth_z, index_x, index_y, index_z):
    along_z = select_apply(smooth_z, index_z, jacobian, "zw,mxyw->mxyz", (1, NX, NY, 1))
    along_y = select_apply(smooth_y, index_y, along_z, "yv,mxvz->mxyz", (1, NX, 1, NZ))
    smoothed = select_apply(smooth_x, index_x, along_y, "xu,muyz->mxyz", (1, 1, NY, NZ))
    panel = smoothed.reshape(M, NX * NY * NZ).astype(jnp.bfloat16)
    widened = panel.astype(jnp.float32)
    return lax.dot_general(widened, widened, (((1,), (1,)), ((), ())), precision=lax.Precision.HIGHEST, preferred_element_type=jnp.float32)
```

```python
import functools

import jax
import jax.numpy as jnp
from jax import lax
from jax.experimental import pallas as pl
from jax.experimental.pallas import tpu as pltpu
from jax.sharding import Mesh, PartitionSpec as P

BAND = 3
TAPS = 2 * BAND + 1
TABLES = 4
F32 = jnp.float32
BF16 = jnp.bfloat16
VMEM = pl.BlockSpec(memory_space=pltpu.VMEM)
SMEM = pl.BlockSpec(memory_space=pltpu.SMEM)


def split_table(table):
    high = table.astype(BF16)
    low = (table - high.astype(F32)).astype(BF16)
    return high, low


def band_column(table, tap):
    rows = lax.broadcasted_iota(jnp.int32, table.shape, 0)
    cols = lax.broadcasted_iota(jnp.int32, table.shape, 1)
    return jnp.sum(jnp.where(cols == rows + (tap - BAND), table, 0.0), axis=1, keepdims=True)


def zy_kernel(index_y, index_z, table_y, table_z, jac, out, coef):
    group = pl.program_id(0)
    rows, planes, nz, ny = jac.shape
    lhs = []
    for t in range(TABLES):
        high, low = split_table(table_y[t])
        lhs.append(jnp.concatenate([high, low], axis=1))
    lhs = jnp.concatenate(lhs, axis=0)
    for tap in range(TAPS):
        cols = [band_column(table_z[t], tap) for t in range(TABLES)]
        for x in range(planes):
            label = index_z[pl.ds(group * planes + x, 1), :]
            picked = jnp.broadcast_to(cols[0], (nz, ny))
            for t in range(1, TABLES):
                picked = jnp.where(label == t, cols[t], picked)
            coef[x, tap] = picked
    lane = lax.broadcasted_iota(jnp.int32, (1, planes * rows), 1)
    for z in range(0, nz, 2):
        parts = []
        for zz in (z, z + 1):
            for x in range(planes):
                total = None
                for tap in range(TAPS):
                    w = zz + tap - BAND
                    if 0 <= w < nz:
                        term = coef[x, tap, pl.ds(zz, 1), :] * jac[:, x, w, :]
                        total = term if total is None else total + term
                short = total.astype(BF16)
                parts.append(jnp.concatenate([short, short], axis=1))
        rhs = jnp.concatenate(parts, axis=0)
        both = lax.dot_general(lhs, rhs, (((1,), (1,)), ((), ())), preferred_element_type=F32)
        for k, zz in enumerate((z, z + 1)):
            label = jnp.full_like(lane, index_y[group * planes, zz])
            for x in range(1, planes):
                label = jnp.where(lane >= x * rows, index_y[group * planes + x, zz], label)
            part = both[:, k * planes * rows : (k + 1) * planes * rows]
            picked = part[:ny]
            for t in range(1, TABLES):
                picked = jnp.where(label == t, part[t * ny : (t + 1) * ny], picked)
            out[zz] = picked.astype(BF16)


def smooth_zy(jacobian, smooth_y, smooth_z, index_y, index_z):
    rows, slab, ny, nz = jacobian.shape
    planes = 2
    return pl.pallas_call(
        zy_kernel,
        grid=(slab // planes,),
        out_shape=jax.ShapeDtypeStruct((nz, ny, slab * rows), BF16),
        in_specs=[
            SMEM,
            VMEM,
            VMEM,
            VMEM,
            pl.BlockSpec((rows, planes, nz, ny), lambda i: (0, i, 0, 0)),
        ],
        out_specs=pl.BlockSpec((nz, ny, planes * rows), lambda i: (0, 0, i)),
        scratch_shapes=[pltpu.VMEM((planes, TAPS, nz, ny), F32)],
        compiler_params=pltpu.CompilerParams(vmem_limit_bytes=40 * 2**20),
        name="smooth_zy",
    )(index_y, index_z, smooth_y, smooth_z, jnp.swapaxes(jacobian, 2, 3))


def x_kernel(place, index_x, table_x, got, out, wide, bands):
    z, y0 = place[0], place[1]
    columns = got.shape[1]
    cells, per = 16, 4
    nx = cells * per
    for t in range(TABLES):
        table = table_x[t]
        for tap in range(TAPS):
            bands[t, tap] = jnp.broadcast_to(band_column(table, tap), (nx, 128))
    row = index_x[pl.ds(z, 1), :]
    sub = lax.broadcasted_iota(jnp.int32, (columns, row.shape[1]), 0)
    lan = lax.broadcasted_iota(jnp.int32, (columns, row.shape[1]), 1)
    label = jnp.sum(jnp.where(lan == sub + y0, row, 0).astype(F32), axis=1, keepdims=True)
    label = jnp.broadcast_to(label, (columns, 128))
    left = lax.broadcasted_iota(jnp.int32, (columns, 128), 1) < 64

    for edge in range(BAND):
        wide[edge] = jnp.zeros(wide.shape[1:], F32)
        wide[nx + BAND + edge] = jnp.zeros(wide.shape[1:], F32)

    @pl.loop(0, cells)
    def _(cell):
        for parity in range(2):
            for zh in range(2):
                first = (zh * 4 + parity) * cells + cell
                second = (zh * 4 + 2 + parity) * cells + cell
                lanes = pl.ds((parity * 2 + zh) * 128, 128)
                for pair in range(per // 2):
                    a = got[first, :, pl.ds(pair * 128, 128)].astype(F32)
                    b = got[second, :, pl.ds(pair * 128, 128)].astype(F32)
                    base = cell * per + pair * 2 + BAND
                    wide[base, :, lanes] = jnp.where(left, a, pltpu.roll(b, 64, 1))
                    wide[base + 1, :, lanes] = jnp.where(left, pltpu.roll(a, 64, 1), b)

    @pl.loop(0, nx)
    def _(x):
        totals = [None] * 4
        for tap in range(TAPS):
            coef = jnp.broadcast_to(bands[0, tap, pl.ds(x, 1), :], label.shape)
            for t in range(1, TABLES):
                coef = jnp.where(label == t, bands[t, tap, pl.ds(x, 1), :], coef)
            for block in range(4):
                term = coef * wide[x + tap, :, pl.ds(block * 128, 128)]
                totals[block] = term if tap == 0 else totals[block] + term
        for block in range(4):
            out[x, :, pl.ds(block * 128, 128)] = totals[block].astype(BF16)


def smooth_x_local(got, smooth_x, index_x, place):
    columns = got.shape[1]
    nx = smooth_x.shape[1]
    return pl.pallas_call(
        x_kernel,
        out_shape=jax.ShapeDtypeStruct((nx, columns, 512), BF16),
        in_specs=[SMEM, VMEM, VMEM, VMEM],
        out_specs=VMEM,
        scratch_shapes=[
            pltpu.VMEM((nx + 2 * BAND, columns, 512), F32),
            pltpu.VMEM((TABLES, TAPS, nx, 128), F32),
        ],
        compiler_params=pltpu.CompilerParams(vmem_limit_bytes=40 * 2**20),
        name="smooth_x",
    )(place, jnp.swapaxes(index_x, 0, 1), smooth_x, got)


def gram_kernel(core, own, other, out):
    mine = core[0]
    left = own[...]
    for k, right in enumerate((own, other)):
        which = mine if k == 0 else 1 - mine
        for part in range(2):
            piece = lax.dot_general(
                left,
                right[:, part * 256 : (part + 1) * 256],
                (((0,), (0,)), ((), ())),
                preferred_element_type=F32,
            ).astype(BF16)
            for x in range(4):
                for zh in range(2):
                    start = ((x % 2 * 2 + zh) * 2 + x // 2) * 64
                    out[x, part * 2 + which, pl.ds(zh * 64, 64), :] = piece[start : start + 64]


def gram(core, own, other):
    return pl.pallas_call(
        gram_kernel,
        out_shape=jax.ShapeDtypeStruct((4, 4, 128, 256), BF16),
        in_specs=[SMEM, VMEM, VMEM],
        out_specs=VMEM,
        compiler_params=pltpu.CompilerParams(vmem_limit_bytes=40 * 2**20),
        name="gram",
    )(core, own, other)


def sum_plane_kernel(got, out):
    total = got[0].astype(F32)
    for k in range(1, got.shape[0]):
        total = total + got[k].astype(F32)
    for zh in range(2):
        for zl in range(4):
            block = total[zh * 64 : (zh + 1) * 64, zl * 64 : (zl + 1) * 64]
            out[zh * 4 + zl] = jnp.concatenate([block[:32], block[32:]], axis=1)


def sum_plane(got):
    return pl.pallas_call(
        sum_plane_kernel,
        out_shape=jax.ShapeDtypeStruct((8, 32, 128), F32),
        in_specs=[VMEM],
        out_specs=VMEM,
        name="sum_plane",
    )(got)


def sum_line_kernel(got, out):
    total = got[0]
    for k in range(1, got.shape[0]):
        total = total + got[k]
    out[pl.ds(0, 32), :] = total[:, :64]
    out[pl.ds(32, 32), :] = total[:, 64:]


def sum_line(got):
    return pl.pallas_call(
        sum_line_kernel,
        out_shape=jax.ShapeDtypeStruct((64, 64), F32),
        in_specs=[VMEM],
        out_specs=VMEM,
        name="sum_line",
    )(got)


def body(jacobian, smooth_x, smooth_y, smooth_z, index_x, index_y, index_z):
    sent = smooth_zy(jacobian, smooth_y, smooth_z, index_y, index_z)
    nz, ny, width = sent.shape
    got = lax.all_to_all(
        sent.reshape(128, nz * ny // 128, width), ("zh", "x", "zl", "y"), 0, 0, tiled=True
    )
    z = lax.axis_index(("zh", "x", "zl"))
    y0 = lax.axis_index("y") * 16
    core = lax.axis_index("core")
    panel = smooth_x_local(got, smooth_x, index_x, jnp.stack([z, y0]).astype(jnp.int32))
    own = panel.reshape(-1, panel.shape[2])
    other = lax.ppermute(own, "core", [(0, 1), (1, 0)])
    partial = gram(core.reshape(1).astype(jnp.int32), own, other)
    plane = lax.all_to_all(partial.reshape(16, 128, 256), ("x", "y"), 0, 0, tiled=True)
    line = lax.all_to_all(sum_plane(plane), ("zh", "zl"), 0, 0, tiled=True)
    return sum_line(line)


def solution(mesh):
    fine = Mesh(mesh.devices.reshape(2, 4, 2, 4, 4), ("zh", "x", "core", "zl", "y"))
    rows, cells = ("zh", "x", "core"), ("zl", "y")
    return jax.shard_map(
        body,
        mesh=fine,
        in_specs=(
            P(rows, cells, None, None),
            P(),
            P(),
            P(),
            P(),
            P(cells, None),
            P(cells, None),
        ),
        out_specs=P(rows, cells),
        check_vma=False,
    )
```

```python
import functools

import jax
import jax.numpy as jnp
from jax import lax
from jax.experimental import pallas as pl
from jax.experimental.pallas import tpu as pltpu
from jax.sharding import Mesh, PartitionSpec as P

BAND = 3
TAPS = 2 * BAND + 1
TABLES = 4
F32 = jnp.float32
BF16 = jnp.bfloat16
VMEM = pl.BlockSpec(memory_space=pltpu.VMEM)
SMEM = pl.BlockSpec(memory_space=pltpu.SMEM)


def split_table(table):
    high = table.astype(BF16)
    low = (table - high.astype(F32)).astype(BF16)
    return high, low


def band_column(table, tap):
    rows = lax.broadcasted_iota(jnp.int32, table.shape, 0)
    cols = lax.broadcasted_iota(jnp.int32, table.shape, 1)
    return jnp.sum(jnp.where(cols == rows + (tap - BAND), table, 0.0), axis=1, keepdims=True)


def zy_kernel(index_y, index_z, table_y, table_z, jac, out, coef):
    group = pl.program_id(0)
    rows, planes, nz, ny = jac.shape
    lhs = []
    for t in range(TABLES):
        high, low = split_table(table_y[t])
        lhs.append(jnp.concatenate([high, low], axis=1))
    lhs = jnp.concatenate(lhs, axis=0)
    for tap in range(TAPS):
        cols = [band_column(table_z[t], tap) for t in range(TABLES)]
        for x in range(planes):
            label = index_z[pl.ds(group * planes + x, 1), :]
            picked = jnp.broadcast_to(cols[0], (nz, ny))
            for t in range(1, TABLES):
                picked = jnp.where(label == t, cols[t], picked)
            coef[x, tap] = picked
    lane = lax.broadcasted_iota(jnp.int32, (1, planes * rows), 1)
    for z in range(0, nz, 2):
        parts = []
        for zz in (z, z + 1):
            for x in range(planes):
                total = None
                for tap in range(TAPS):
                    w = zz + tap - BAND
                    if 0 <= w < nz:
                        term = coef[x, tap, pl.ds(zz, 1), :] * jac[:, x, w, :]
                        total = term if total is None else total + term
                short = total.astype(BF16)
                parts.append(jnp.concatenate([short, short], axis=1))
        rhs = jnp.concatenate(parts, axis=0)
        both = lax.dot_general(lhs, rhs, (((1,), (1,)), ((), ())), preferred_element_type=F32)
        for k, zz in enumerate((z, z + 1)):
            label = jnp.full_like(lane, index_y[group * planes, zz])
            for x in range(1, planes):
                label = jnp.where(lane >= x * rows, index_y[group * planes + x, zz], label)
            part = both[:, k * planes * rows : (k + 1) * planes * rows]
            picked = part[:ny]
            for t in range(1, TABLES):
                picked = jnp.where(label == t, part[t * ny : (t + 1) * ny], picked)
            out[zz] = picked.astype(BF16)


def smooth_zy(jacobian, smooth_y, smooth_z, index_y, index_z):
    rows, slab, ny, nz = jacobian.shape
    planes = 2
    return pl.pallas_call(
        zy_kernel,
        grid=(slab // planes,),
        out_shape=jax.ShapeDtypeStruct((nz, ny, slab * rows), BF16),
        in_specs=[
            SMEM,
            VMEM,
            VMEM,
            VMEM,
            pl.BlockSpec((rows, planes, nz, ny), lambda i: (0, i, 0, 0)),
        ],
        out_specs=pl.BlockSpec((nz, ny, planes * rows), lambda i: (0, 0, i)),
        scratch_shapes=[pltpu.VMEM((planes, TAPS, nz, ny), F32)],
        compiler_params=pltpu.CompilerParams(vmem_limit_bytes=40 * 2**20),
        name="smooth_zy",
    )(index_y, index_z, smooth_y, smooth_z, jnp.swapaxes(jacobian, 2, 3))


def x_kernel(place, index_x, table_x, got, out, wide, bands):
    z, y0 = place[0], place[1]
    columns = got.shape[1]
    cells, per = 16, 4
    nx = cells * per
    for t in range(TABLES):
        table = table_x[t]
        for tap in range(TAPS):
            bands[t, tap] = jnp.broadcast_to(band_column(table, tap), (nx, 128))
    row = index_x[pl.ds(z, 1), :]
    sub = lax.broadcasted_iota(jnp.int32, (columns, row.shape[1]), 0)
    lan = lax.broadcasted_iota(jnp.int32, (columns, row.shape[1]), 1)
    label = jnp.sum(jnp.where(lan == sub + y0, row, 0).astype(F32), axis=1, keepdims=True)
    label = jnp.broadcast_to(label, (columns, 128))
    left = lax.broadcasted_iota(jnp.int32, (columns, 128), 1) < 64

    for edge in range(BAND):
        wide[edge] = jnp.zeros(wide.shape[1:], F32)
        wide[nx + BAND + edge] = jnp.zeros(wide.shape[1:], F32)

    @pl.loop(0, cells)
    def _(cell):
        for parity in range(2):
            for zh in range(2):
                first = zh * 64 + cell // 4 * 16 + parity * 4 + cell % 4
                second = first + 8
                lanes = pl.ds((parity * 2 + zh) * 128, 128)
                for pair in range(per // 2):
                    a = got[first, :, pl.ds(pair * 128, 128)].astype(F32)
                    b = got[second, :, pl.ds(pair * 128, 128)].astype(F32)
                    base = cell * per + pair * 2 + BAND
                    wide[base, :, lanes] = jnp.where(left, a, pltpu.roll(b, 64, 1))
                    wide[base + 1, :, lanes] = jnp.where(left, pltpu.roll(a, 64, 1), b)

    @pl.loop(0, nx)
    def _(x):
        totals = [None] * 4
        for tap in range(TAPS):
            coef = jnp.broadcast_to(bands[0, tap, pl.ds(x, 1), :], label.shape)
            for t in range(1, TABLES):
                coef = jnp.where(label == t, bands[t, tap, pl.ds(x, 1), :], coef)
            for block in range(4):
                term = coef * wide[x + tap, :, pl.ds(block * 128, 128)]
                totals[block] = term if tap == 0 else totals[block] + term
        for block in range(4):
            out[x, :, pl.ds(block * 128, 128)] = totals[block].astype(BF16)


def smooth_x_local(got, smooth_x, index_x, place):
    columns = got.shape[1]
    nx = smooth_x.shape[1]
    return pl.pallas_call(
        x_kernel,
        out_shape=jax.ShapeDtypeStruct((nx, columns, 512), BF16),
        in_specs=[SMEM, VMEM, VMEM, VMEM],
        out_specs=VMEM,
        scratch_shapes=[
            pltpu.VMEM((nx + 2 * BAND, columns, 512), F32),
            pltpu.VMEM((TABLES, TAPS, nx, 128), F32),
        ],
        compiler_params=pltpu.CompilerParams(vmem_limit_bytes=40 * 2**20),
        name="smooth_x",
    )(place, jnp.swapaxes(index_x, 0, 1), smooth_x, got)


def gram_kernel(core, own, other, out):
    mine = core[0]
    left = own[...]
    low = lax.broadcasted_iota(jnp.int32, (32, 128), 1) < 64
    for k, right in enumerate((own, other)):
        which = mine if k == 0 else 1 - mine
        for part in range(2):
            whole = lax.dot_general(
                left,
                right[:, part * 256 : (part + 1) * 256],
                (((0,), (0,)), ((), ())),
                preferred_element_type=F32,
            )
            for x in range(4):
                for zh in range(2):
                    start = ((x % 2 * 2 + zh) * 2 + x // 2) * 64
                    for pair in range(2):
                        lanes = slice(pair * 128, pair * 128 + 128)
                        upper = whole[start : start + 32, lanes]
                        lower = whole[start + 32 : start + 64, lanes]
                        first = jnp.where(low, upper, pltpu.roll(lower, 64, 1))
                        second = jnp.where(low, pltpu.roll(upper, 64, 1), lower)
                        out[zh, pair * 2, x, part * 2 + which] = first.astype(BF16)
                        out[zh, pair * 2 + 1, x, part * 2 + which] = second.astype(BF16)


def gram(core, own, other):
    return pl.pallas_call(
        gram_kernel,
        out_shape=jax.ShapeDtypeStruct((2, 4, 4, 4, 32, 128), BF16),
        in_specs=[SMEM, VMEM, VMEM],
        out_specs=VMEM,
        compiler_params=pltpu.CompilerParams(vmem_limit_bytes=40 * 2**20),
        name="gram",
    )(core, own, other)


def sum_kernel(got, out):
    total = got[0].astype(F32)
    for k in range(1, got.shape[0]):
        total = total + got[k].astype(F32)
    out[pl.ds(0, 32), :] = total[:, :64]
    out[pl.ds(32, 32), :] = total[:, 64:]


def sum_parts(got):
    return pl.pallas_call(
        sum_kernel,
        out_shape=jax.ShapeDtypeStruct((64, 64), F32),
        in_specs=[VMEM],
        out_specs=VMEM,
        name="sum_parts",
    )(got)


def body(jacobian, smooth_x, smooth_y, smooth_z, index_x, index_y, index_z):
    chips = ("zh", "zl", "x", "y")
    sent = smooth_zy(jacobian, smooth_y, smooth_z, index_y, index_z)
    nz, ny, width = sent.shape
    got = lax.all_to_all(sent.reshape(128, nz * ny // 128, width), chips, 0, 0, tiled=True)
    z = lax.axis_index(("zh", "zl", "x"))
    y0 = lax.axis_index("y") * 16
    core = lax.axis_index("core")
    panel = smooth_x_local(got, smooth_x, index_x, jnp.stack([z, y0]).astype(jnp.int32))
    own = panel.reshape(-1, panel.shape[2])
    other = lax.ppermute(own, "core", [(0, 1), (1, 0)])
    partial = gram(core.reshape(1).astype(jnp.int32), own, other)
    parts = lax.all_to_all(partial.reshape(128, 32, 128), chips, 0, 0, tiled=True)
    return sum_parts(parts)


def solution(mesh):
    fine = Mesh(mesh.devices.reshape(2, 4, 2, 4, 4), ("zh", "x", "core", "zl", "y"))
    rows, cells = ("zh", "x", "core"), ("zl", "y")
    return jax.shard_map(
        body,
        mesh=fine,
        in_specs=(
            P(rows, cells, None, None),
            P(),
            P(),
            P(),
            P(),
            P(cells, None),
            P(cells, None),
        ),
        out_specs=P(rows, cells),
        check_vma=False,
    )
```

```python
import jax
import jax.numpy as jnp
from jax import lax
from jax.experimental import pallas as pl
from jax.experimental.pallas import tpu as pltpu
from jax.sharding import Mesh, PartitionSpec as P

BAND = 3
TAPS = 2 * BAND + 1
TABLES = 4
GROUP = 8
AHEAD = 3
F32 = jnp.float32
BF16 = jnp.bfloat16
VMEM = pl.BlockSpec(memory_space=pltpu.VMEM)
SMEM = pl.BlockSpec(memory_space=pltpu.SMEM)
HBM = pl.BlockSpec(memory_space=pltpu.HBM)


def split_table(table):
    high = table.astype(BF16)
    low = (table - high.astype(F32)).astype(BF16)
    return high, low


def band_column(table, tap):
    rows = lax.broadcasted_iota(jnp.int32, table.shape, 0)
    cols = lax.broadcasted_iota(jnp.int32, table.shape, 1)
    return jnp.sum(jnp.where(cols == rows + (tap - BAND), table, 0.0), axis=1, keepdims=True)


def zy_kernel(jac, table_y, table_z, index_y, index_z, out, planes, coef, lhs, ty, tz, iy, iz, sems, small):
    slab, nz, rows, ny = planes.shape
    loads = [
        pltpu.make_async_copy(s, d, small.at[k])
        for k, (s, d) in enumerate(((table_z, tz), (index_z, iz), (table_y, ty), (index_y, iy)))
    ]
    for load in loads:
        load.start()
    waves = []
    for x0 in range(0, slab, 2):
        for w0 in range(0, nz, GROUP):
            waves.append([(x, w) for w in range(w0, w0 + GROUP) for x in (x0, x0 + 1)])
    copies = {}
    started, waited = [0], [0]

    def start_until(count):
        while started[0] < min(count, len(waves)):
            for x, w in waves[started[0]]:
                copies[x, w] = pltpu.make_async_copy(jac.at[:, x, w, :], planes.at[x, w], sems.at[x, w])
                copies[x, w].start()
            started[0] += 1

    def wait_until(count):
        while waited[0] < min(count, len(waves)):
            for x, w in waves[waited[0]]:
                copies[x, w].wait()
            waited[0] += 1

    start_until(AHEAD)
    loads[0].wait()
    loads[1].wait()
    for tap in range(TAPS):
        cols = [band_column(tz[t], tap) for t in range(TABLES)]
        for x in range(slab):
            label = iz[pl.ds(x, 1), :]
            picked = jnp.broadcast_to(cols[0], (nz, ny))
            for t in range(1, TABLES):
                picked = jnp.where(label == t, cols[t], picked)
            coef[x, tap] = picked
    loads[2].wait()
    loads[3].wait()
    for t in range(TABLES):
        high, low = split_table(ty[t])
        lhs[pl.ds(t * ny, ny), :] = jnp.concatenate([high, low], axis=1)
    left = lhs[...]
    lane = lax.broadcasted_iota(jnp.int32, (1, 2 * rows), 1)
    half = rows // 2

    def finish(both, z, x0):
        for k, zz in enumerate((z, z + 1)):
            label = jnp.where(lane < rows, iy[x0, zz], iy[x0 + 1, zz])
            part = both[:, k * 2 * rows : (k + 1) * 2 * rows]
            picked = part[:ny]
            for t in range(1, TABLES):
                picked = jnp.where(label == t, part[t * ny : (t + 1) * ny], picked)
            out[zz, :, pl.ds(x0 * rows, 2 * rows)] = picked.astype(BF16)

    pending = []
    for x0 in range(0, slab, 2):
        for z in range(0, nz, 2):
            per = nz // GROUP
            need = x0 // 2 * per + min(z + BAND + 1, nz - 1) // GROUP + 1
            start_until(need + AHEAD - 1)
            wait_until(need)
            parts = {}
            for x in (x0, x0 + 1):
                for h in range(2):
                    use = pl.ds(h * half, half)
                    held = {w: planes[x, w, use, :] for w in range(max(z - BAND, 0), min(z + BAND + 2, nz))}
                    for zz in (z, z + 1):
                        total = None
                        for w in range(max(zz - BAND, 0), min(zz + BAND + 1, nz)):
                            term = coef[x, w - zz + BAND, pl.ds(zz, 1), :] * held[w]
                            total = term if total is None else total + term
                        short = total.astype(BF16)
                        parts[zz, x, h] = jnp.concatenate([short, short], axis=1)
            rhs = jnp.concatenate([parts[zz, x, h] for zz in (z, z + 1) for x in (x0, x0 + 1) for h in range(2)], axis=0)
            both = lax.dot_general(left, rhs, (((1,), (1,)), ((), ())), preferred_element_type=F32)
            pending.append((both, z, x0))
            if len(pending) > 1:
                finish(*pending.pop(0))
    for item in pending:
        finish(*item)


def smooth_zy(jacobian, smooth_y, smooth_z, index_y, index_z):
    rows, slab, ny, nz = jacobian.shape
    return pl.pallas_call(
        zy_kernel,
        out_shape=jax.ShapeDtypeStruct((nz, ny, slab * rows), BF16),
        in_specs=[HBM] * 5,
        out_specs=VMEM,
        scratch_shapes=[
            pltpu.VMEM((slab, nz, rows, ny), F32),
            pltpu.VMEM((slab, TAPS, nz, ny), F32),
            pltpu.VMEM((TABLES * ny, 2 * ny), BF16),
            pltpu.VMEM(smooth_y.shape, F32),
            pltpu.VMEM(smooth_z.shape, F32),
            pltpu.SMEM(index_y.shape, jnp.int32),
            pltpu.VMEM(index_z.shape, jnp.int32),
            pltpu.SemaphoreType.DMA((slab, nz)),
            pltpu.SemaphoreType.DMA((4,)),
        ],
        compiler_params=pltpu.CompilerParams(vmem_limit_bytes=60 * 2**20),
        name="smooth_zy",
    )(jnp.swapaxes(jacobian, 2, 3), smooth_y, smooth_z, index_y, index_z)


def coef_kernel(place, index_x, table_x, out, bands):
    z, y0 = place[0], place[1]
    nx, taps, columns, lanes = out.shape
    for t in range(TABLES):
        for tap in range(taps):
            bands[t, tap] = jnp.broadcast_to(band_column(table_x[t], tap), (nx, lanes))
    row = index_x[pl.ds(z, 1), :]
    sub = lax.broadcasted_iota(jnp.int32, (columns, row.shape[1]), 0)
    lan = lax.broadcasted_iota(jnp.int32, (columns, row.shape[1]), 1)
    label = jnp.sum(jnp.where(lan == sub + y0, row, 0).astype(F32), axis=1, keepdims=True)
    label = jnp.broadcast_to(label, (columns, lanes))

    @pl.loop(0, nx)
    def _(x):
        for tap in range(taps):
            picked = jnp.broadcast_to(bands[0, tap, pl.ds(x, 1), :], label.shape)
            for t in range(1, TABLES):
                picked = jnp.where(label == t, bands[t, tap, pl.ds(x, 1), :], picked)
            out[x, tap] = picked


def x_coefs(place, index_x, smooth_x):
    nx = smooth_x.shape[1]
    return pl.pallas_call(
        coef_kernel,
        out_shape=jax.ShapeDtypeStruct((nx, TAPS, 16, 128), F32),
        in_specs=[SMEM, VMEM, VMEM],
        out_specs=VMEM,
        scratch_shapes=[pltpu.VMEM((TABLES, TAPS, nx, 128), F32)],
        compiler_params=pltpu.CompilerParams(vmem_limit_bytes=12 * 2**20),
        cost_estimate=pl.CostEstimate(flops=4 * 2**20, bytes_accessed=4 * 2**20, transcendentals=0),
        name="x_coefs",
    )(place, jnp.swapaxes(index_x, 0, 1), smooth_x)


def x_kernel(coef, got, out, wide):
    nx, columns, lanes = out.shape
    left = lax.broadcasted_iota(jnp.int32, (columns, 128), 1) < 64
    for edge in range(BAND):
        wide[edge] = jnp.zeros(wide.shape[1:], F32)
        wide[nx + BAND + edge] = jnp.zeros(wide.shape[1:], F32)

    def merge(cell, carry):
        for parity in range(2):
            for zh in range(2):
                first = zh * 64 + cell // 4 * 16 + parity * 4 + cell % 4
                second = first + 8
                use = pl.ds((parity * 2 + zh) * 128, 128)
                for pair in range(2):
                    a = got[first, :, pl.ds(pair * 128, 128)].astype(F32)
                    b = got[second, :, pl.ds(pair * 128, 128)].astype(F32)
                    base = cell * 4 + pair * 2 + BAND
                    wide[base, :, use] = jnp.where(left, a, pltpu.roll(b, 64, 1))
                    wide[base + 1, :, use] = jnp.where(left, pltpu.roll(a, 64, 1), b)
        return carry

    def smooth(step, carry):
        x = step * 2
        for block in range(lanes // 128):
            use = pl.ds(block * 128, 128)
            held = [wide[x + k, :, use] for k in range(TAPS + 1)]
            for k in range(2):
                total = coef[x + k, 0] * held[k]
                for tap in range(1, TAPS):
                    total = total + coef[x + k, tap] * held[k + tap]
                out[x + k, :, use] = total.astype(BF16)
        return carry

    lax.fori_loop(0, nx // 4, merge, 0, unroll=16)
    lax.fori_loop(0, nx // 2, smooth, 0, unroll=8)


def smooth_x_local(coef, got):
    nx, _, columns, _ = coef.shape
    return pl.pallas_call(
        x_kernel,
        out_shape=jax.ShapeDtypeStruct((nx, columns, 512), BF16),
        in_specs=[VMEM, VMEM],
        out_specs=VMEM,
        scratch_shapes=[pltpu.VMEM((nx + 2 * BAND, columns, 512), F32)],
        compiler_params=pltpu.CompilerParams(vmem_limit_bytes=12 * 2**20),
        name="smooth_x",
    )(coef, got)


def add_up(parts):
    while len(parts) > 1:
        parts = [a + b for a, b in zip(parts[::2], parts[1::2])] + parts[len(parts) // 2 * 2 :]
    return parts[0]


def gram_kernel(core, own, other, out):
    mine = core[0]
    left = own[...]
    for k, right in enumerate((own, other)):
        which = mine if k == 0 else 1 - mine
        for part in range(2):
            piece = lax.dot_general(
                left,
                right[:, part * 256 : (part + 1) * 256],
                (((0,), (0,)), ((), ())),
                preferred_element_type=F32,
            ).astype(BF16)
            for x in range(4):
                for zh in range(2):
                    start = ((x % 2 * 2 + zh) * 2 + x // 2) * 64
                    out[x, part * 2 + which, pl.ds(zh * 64, 64), :] = piece[start : start + 64]


def gram(core, own, other):
    return pl.pallas_call(
        gram_kernel,
        out_shape=jax.ShapeDtypeStruct((4, 4, 128, 256), BF16),
        in_specs=[SMEM, VMEM, VMEM],
        out_specs=VMEM,
        compiler_params=pltpu.CompilerParams(vmem_limit_bytes=16 * 2**20),
        name="gram",
    )(core, own, other)


def sum_plane_kernel(got, out):
    for zh in range(2):
        for pair in range(2):
            rows, lanes = pl.ds(zh * 64, 64), pl.ds(pair * 128, 128)
            total = add_up([got[k, rows, lanes].astype(F32) for k in range(got.shape[0])])
            left = lax.broadcasted_iota(jnp.int32, (32, 128), 1) < 64
            upper, lower = total[:32], total[32:]
            out[zh * 4 + pair * 2] = jnp.where(left, upper, pltpu.roll(lower, 64, 1))
            out[zh * 4 + pair * 2 + 1] = jnp.where(left, pltpu.roll(upper, 64, 1), lower)


def sum_plane(got):
    return pl.pallas_call(
        sum_plane_kernel,
        out_shape=jax.ShapeDtypeStruct((8, 32, 128), F32),
        in_specs=[VMEM],
        out_specs=VMEM,
        compiler_params=pltpu.CompilerParams(vmem_limit_bytes=8 * 2**20),
        name="sum_plane",
    )(got)


def sum_line_kernel(got, out):
    total = add_up([got[k] for k in range(got.shape[0])])
    out[pl.ds(0, 32), :] = total[:, :64]
    out[pl.ds(32, 32), :] = total[:, 64:]


def sum_line(got):
    return pl.pallas_call(
        sum_line_kernel,
        out_shape=jax.ShapeDtypeStruct((64, 64), F32),
        in_specs=[VMEM],
        out_specs=VMEM,
        compiler_params=pltpu.CompilerParams(vmem_limit_bytes=4 * 2**20),
        name="sum_line",
    )(got)


def body(jacobian, smooth_x, smooth_y, smooth_z, index_x, index_y, index_z):
    sent = smooth_zy(jacobian, smooth_y, smooth_z, index_y, index_z)
    nz, ny, width = sent.shape
    place = jnp.stack([lax.axis_index(("zh", "zl", "x")), lax.axis_index("y") * 16]).astype(jnp.int32)
    coef = x_coefs(place, index_x, smooth_x)
    got = lax.all_to_all(
        sent.reshape(128, nz * ny // 128, width), ("zh", "zl", "x", "y"), 0, 0, tiled=True
    )
    panel = smooth_x_local(coef, got)
    own = panel.reshape(-1, panel.shape[2])
    other = lax.ppermute(own, "core", [(0, 1), (1, 0)])
    core = lax.axis_index("core").reshape(1).astype(jnp.int32)
    partial = gram(core, own, other)
    plane = lax.all_to_all(partial.reshape(16, 128, 256), ("x", "y"), 0, 0, tiled=True)
    line = lax.all_to_all(sum_plane(plane), ("zh", "zl"), 0, 0, tiled=True)
    return sum_line(line)


def solution(mesh):
    fine = Mesh(mesh.devices.reshape(2, 4, 2, 4, 4), ("zh", "x", "core", "zl", "y"))
    rows, cells = ("zh", "x", "core"), ("zl", "y")
    return jax.shard_map(
        body,
        mesh=fine,
        in_specs=(
            P(rows, cells, None, None),
            P(),
            P(),
            P(),
            P(),
            P(cells, None),
            P(cells, None),
        ),
        out_specs=P(rows, cells),
        check_vma=False,
    )
```

```python
import jax
import jax.numpy as jnp
from jax import lax
from jax.experimental import pallas as pl
from jax.experimental.pallas import tpu as pltpu
from jax.sharding import Mesh, PartitionSpec as P

BAND = 3
TAPS = 2 * BAND + 1
TABLES = 4
GROUP = 8
AHEAD = 3
F32 = jnp.float32
BF16 = jnp.bfloat16
VMEM = pl.BlockSpec(memory_space=pltpu.VMEM)
SMEM = pl.BlockSpec(memory_space=pltpu.SMEM)
HBM = pl.BlockSpec(memory_space=pltpu.HBM)


def split_table(table):
    high = table.astype(BF16)
    low = (table - high.astype(F32)).astype(BF16)
    return high, low


def band_column(table, tap):
    rows = lax.broadcasted_iota(jnp.int32, table.shape, 0)
    cols = lax.broadcasted_iota(jnp.int32, table.shape, 1)
    return jnp.sum(jnp.where(cols == rows + (tap - BAND), table, 0.0), axis=1, keepdims=True)


def zy_kernel(jac, table_y, table_z, index_y, index_z, out, planes, coef, lhs, done, ty, tz, iy, iz, sems, outs, small):
    slab, _, rows, ny = planes.shape
    nz = done.shape[0]
    per = nz // GROUP
    steps = slab // 2 * per
    loads = [
        pltpu.make_async_copy(s, d, small.at[k])
        for k, (s, d) in enumerate(((table_z, tz), (index_z, iz), (table_y, ty), (index_y, iy)))
    ]
    for load in loads:
        load.start()

    def wave(step):
        pair, group = step // per, step % per
        for k in range(GROUP):
            for x in range(2):
                w = group * GROUP + k
                yield pltpu.make_async_copy(
                    jac.at[:, pair * 2 + x, w, :], planes.at[pair * 2 + x, w + BAND], sems.at[pair * 2 + x, w]
                )

    def result(step):
        pair, group = step // per, step % per
        place = (pl.ds(group * GROUP, GROUP), slice(None), pl.ds(pair * 2 * rows, 2 * rows))
        return pltpu.make_async_copy(done.at[place], out.at[place], outs.at[step])

    for step in range(AHEAD):
        for copy in wave(step):
            copy.start()
    for x in range(slab):
        for edge in range(BAND):
            planes[x, edge] = jnp.zeros((rows, ny), F32)
            planes[x, nz + BAND + edge] = jnp.zeros((rows, ny), F32)
    loads[0].wait()
    loads[1].wait()
    for tap in range(TAPS):
        cols = [band_column(tz[t], tap) for t in range(TABLES)]
        for x in range(slab):
            label = iz[pl.ds(x, 1), :]
            picked = jnp.broadcast_to(cols[0], (nz, ny))
            for t in range(1, TABLES):
                picked = jnp.where(label == t, cols[t], picked)
            coef[x, tap] = picked
    loads[2].wait()
    loads[3].wait()
    split = [split_table(ty[t]) for t in range(TABLES)]
    for t in range(TABLES):
        for u in range(TABLES):
            pieces = [split[t][0], split[u][0], split[t][1], split[u][1]]
            lhs[t * TABLES + u] = jnp.concatenate(pieces, axis=1)
    half = rows // 2
    for copy in wave(0):
        copy.wait()

    for step in range(steps):
        x0, group = step // per * 2, step % per

        if step + AHEAD < steps:
            for copy in wave(step + AHEAD):
                copy.start()
        if step + 1 < steps:
            for copy in wave(step + 1):
                copy.wait()

        parts = {}
        for x in range(2):
            for h in range(2):
                use = pl.ds(h * half, half)
                for k0 in range(0, GROUP, 2):
                    held = [planes[x0 + x, group * GROUP + k0 + j, use, :] for j in range(TAPS + 1)]
                    for k in range(2):
                        z = group * GROUP + k0 + k
                        total = coef[x0 + x, 0, pl.ds(z, 1), :] * held[k]
                        for tap in range(1, TAPS):
                            total = total + coef[x0 + x, tap, pl.ds(z, 1), :] * held[k + tap]
                        short = total.astype(BF16)
                        blank = jnp.zeros_like(short)
                        parts[k0 + k, x, h] = jnp.concatenate([blank, short] if x else [short, blank], axis=1)
        for k in range(GROUP):
            z = group * GROUP + k
            rhs = jnp.concatenate([parts[k, x, h] for x in range(2) for h in range(2)], axis=0)
            both = lax.dot_general(
                lhs[iy[x0, z] * TABLES + iy[x0 + 1, z]],
                jnp.concatenate([rhs, rhs], axis=1),
                (((1,), (1,)), ((), ())),
                preferred_element_type=F32,
            )
            done[z, :, pl.ds(x0 * rows, 2 * rows)] = both.astype(BF16)
        result(step).start()

    for step in range(steps):
        result(step).wait()


def smooth_zy(jacobian, smooth_y, smooth_z, index_y, index_z):
    rows, slab, ny, nz = jacobian.shape
    return pl.pallas_call(
        zy_kernel,
        out_shape=jax.ShapeDtypeStruct((nz, ny, slab * rows), BF16),
        in_specs=[HBM] * 5,
        out_specs=HBM,
        scratch_shapes=[
            pltpu.VMEM((slab, nz + 2 * BAND, rows, ny), F32),
            pltpu.VMEM((slab, TAPS, nz, ny), F32),
            pltpu.VMEM((TABLES * TABLES, ny, 4 * ny), BF16),
            pltpu.VMEM((nz, ny, slab * rows), BF16),
            pltpu.VMEM(smooth_y.shape, F32),
            pltpu.VMEM(smooth_z.shape, F32),
            pltpu.SMEM(index_y.shape, jnp.int32),
            pltpu.VMEM(index_z.shape, jnp.int32),
            pltpu.SemaphoreType.DMA((slab, nz)),
            pltpu.SemaphoreType.DMA((slab // 2 * nz // GROUP,)),
            pltpu.SemaphoreType.DMA((4,)),
        ],
        compiler_params=pltpu.CompilerParams(vmem_limit_bytes=60 * 2**20),
        name="smooth_zy",
    )(jnp.swapaxes(jacobian, 2, 3), smooth_y, smooth_z, index_y, index_z)


def coef_kernel(place, index_x, table_x, out, bands):
    z, y0 = place[0], place[1]
    nx = table_x.shape[1]
    _, columns, lanes = out.shape
    for t in range(TABLES):
        for tap in range(TAPS):
            bands[t, tap] = jnp.broadcast_to(band_column(table_x[t], tap), (nx, lanes))
    row = index_x[pl.ds(z, 1), :]
    sub = lax.broadcasted_iota(jnp.int32, (columns, row.shape[1]), 0)
    lan = lax.broadcasted_iota(jnp.int32, (columns, row.shape[1]), 1)
    label = jnp.sum(jnp.where(lan == sub + y0, row, 0).astype(F32), axis=1, keepdims=True)
    label = jnp.broadcast_to(label, (columns, lanes))

    lane = lax.broadcasted_iota(jnp.int32, label.shape, 1)

    @pl.loop(0, out.shape[0])
    def _(cell):
        total = jnp.zeros(label.shape, F32)
        for k in range(4):
            for tap in range(TAPS):
                row = pl.ds(cell * 4 + k, 1)
                picked = jnp.broadcast_to(bands[0, tap, row, :], label.shape)
                for t in range(1, TABLES):
                    picked = jnp.where(label == t, bands[t, tap, row, :], picked)
                total = jnp.where(lane == k * TAPS + tap, picked, total)
        out[cell] = total


def x_coefs(place, index_x, smooth_x):
    nx = smooth_x.shape[1]
    return pl.pallas_call(
        coef_kernel,
        out_shape=jax.ShapeDtypeStruct((nx // 4, 16, 128), F32),
        in_specs=[SMEM, VMEM, VMEM],
        out_specs=VMEM,
        scratch_shapes=[pltpu.VMEM((TABLES, TAPS, nx, 128), F32)],
        compiler_params=pltpu.CompilerParams(vmem_limit_bytes=12 * 2**20),
        cost_estimate=pl.CostEstimate(flops=4 * 2**20, bytes_accessed=4 * 2**20, transcendentals=0),
        name="x_coefs",
    )(place, jnp.swapaxes(index_x, 0, 1), smooth_x)


def x_kernel(coef, got, out, wide):
    nx, columns, lanes = out.shape
    left = lax.broadcasted_iota(jnp.int32, (columns, 128), 1) < 64
    for edge in range(BAND):
        wide[edge] = jnp.zeros(wide.shape[1:], F32)
        wide[nx + BAND + edge] = jnp.zeros(wide.shape[1:], F32)

    def merge(cell, carry):
        for parity in range(2):
            for zh in range(2):
                first = zh * 64 + cell // 4 * 16 + parity * 4 + cell % 4
                use = pl.ds((parity * 2 + zh) * 128, 128)
                for pair in range(2):
                    a = got[first, :, pl.ds(pair * 128, 128)].astype(F32)
                    b = got[first + 8, :, pl.ds(pair * 128, 128)].astype(F32)
                    base = cell * 4 + pair * 2 + BAND
                    wide[base, :, use] = jnp.where(left, a, pltpu.roll(b, 64, 1))
                    wide[base + 1, :, use] = jnp.where(left, pltpu.roll(a, 64, 1), b)
        return carry

    def smooth(cell, carry):
        taps = coef[cell]
        for k in range(4):
            x = cell * 4 + k
            totals = [None] * (lanes // 128)
            for tap in range(TAPS):
                column = k * TAPS + tap
                factor = jnp.broadcast_to(taps[:, column : column + 1], (columns, 128))
                for block in range(lanes // 128):
                    term = factor * wide[x + tap, :, pl.ds(block * 128, 128)]
                    totals[block] = term if tap == 0 else totals[block] + term
            for block in range(lanes // 128):
                out[x, :, pl.ds(block * 128, 128)] = totals[block].astype(BF16)
        return carry

    lax.fori_loop(0, nx // 4, merge, 0, unroll=16)
    lax.fori_loop(0, nx // 4, smooth, 0, unroll=16)


def smooth_x_local(coef, got):
    nx, columns = coef.shape[0] * 4, coef.shape[1]
    return pl.pallas_call(
        x_kernel,
        out_shape=jax.ShapeDtypeStruct((nx, columns, 512), BF16),
        in_specs=[VMEM, VMEM],
        out_specs=VMEM,
        scratch_shapes=[pltpu.VMEM((nx + 2 * BAND, columns, 512), F32)],
        compiler_params=pltpu.CompilerParams(vmem_limit_bytes=12 * 2**20),
        name="smooth_x",
    )(coef, got)


def add_up(parts):
    while len(parts) > 1:
        parts = [a + b for a, b in zip(parts[::2], parts[1::2])] + parts[len(parts) // 2 * 2 :]
    return parts[0]


def gram_kernel(core, own, other, out):
    mine = core[0]
    left = own[...]
    for k, right in enumerate((own, other)):
        which = mine if k == 0 else 1 - mine
        for part in range(2):
            piece = lax.dot_general(
                left,
                right[:, part * 256 : (part + 1) * 256],
                (((0,), (0,)), ((), ())),
                preferred_element_type=F32,
            ).astype(BF16)
            for x in range(4):
                for zh in range(2):
                    start = ((x % 2 * 2 + zh) * 2 + x // 2) * 64
                    out[x, part * 2 + which, pl.ds(zh * 64, 64), :] = piece[start : start + 64]


def gram(core, own, other):
    return pl.pallas_call(
        gram_kernel,
        out_shape=jax.ShapeDtypeStruct((4, 4, 128, 256), BF16),
        in_specs=[SMEM, VMEM, VMEM],
        out_specs=VMEM,
        compiler_params=pltpu.CompilerParams(vmem_limit_bytes=16 * 2**20),
        name="gram",
    )(core, own, other)


def sum_plane_kernel(got, out):
    for zh in range(2):
        for pair in range(2):
            rows, lanes = pl.ds(zh * 64, 64), pl.ds(pair * 128, 128)
            total = add_up([got[k, rows, lanes].astype(F32) for k in range(got.shape[0])])
            left = lax.broadcasted_iota(jnp.int32, (32, 128), 1) < 64
            upper, lower = total[:32], total[32:]
            out[zh * 4 + pair * 2] = jnp.where(left, upper, pltpu.roll(lower, 64, 1))
            out[zh * 4 + pair * 2 + 1] = jnp.where(left, pltpu.roll(upper, 64, 1), lower)


def sum_plane(got):
    return pl.pallas_call(
        sum_plane_kernel,
        out_shape=jax.ShapeDtypeStruct((8, 32, 128), F32),
        in_specs=[VMEM],
        out_specs=VMEM,
        compiler_params=pltpu.CompilerParams(vmem_limit_bytes=8 * 2**20),
        name="sum_plane",
    )(got)


def sum_line_kernel(got, out):
    total = add_up([got[k] for k in range(got.shape[0])])
    out[pl.ds(0, 32), :] = total[:, :64]
    out[pl.ds(32, 32), :] = total[:, 64:]


def sum_line(got):
    return pl.pallas_call(
        sum_line_kernel,
        out_shape=jax.ShapeDtypeStruct((64, 64), F32),
        in_specs=[VMEM],
        out_specs=VMEM,
        compiler_params=pltpu.CompilerParams(vmem_limit_bytes=4 * 2**20),
        name="sum_line",
    )(got)


def body(jacobian, smooth_x, smooth_y, smooth_z, index_x, index_y, index_z):
    sent = smooth_zy(jacobian, smooth_y, smooth_z, index_y, index_z)
    nz, ny, width = sent.shape
    place = jnp.stack([lax.axis_index(("zh", "zl", "x")), lax.axis_index("y") * 16]).astype(jnp.int32)
    coef = x_coefs(place, index_x, smooth_x)
    got = lax.all_to_all(
        sent.reshape(128, nz * ny // 128, width), ("zh", "zl", "x", "y"), 0, 0, tiled=True
    )
    panel = smooth_x_local(coef, got)
    own = panel.reshape(-1, panel.shape[2])
    other = lax.ppermute(own, "core", [(0, 1), (1, 0)])
    core = lax.axis_index("core").reshape(1).astype(jnp.int32)
    partial = gram(core, own, other)
    plane = lax.all_to_all(partial.reshape(16, 128, 256), ("x", "y"), 0, 0, tiled=True)
    line = lax.all_to_all(sum_plane(plane), ("zh", "zl"), 0, 0, tiled=True)
    return sum_line(line)


def solution(mesh):
    fine = Mesh(mesh.devices.reshape(2, 4, 2, 4, 4), ("zh", "x", "core", "zl", "y"))
    rows, cells = ("zh", "x", "core"), ("zl", "y")
    return jax.shard_map(
        body,
        mesh=fine,
        in_specs=(
            P(rows, cells, None, None),
            P(),
            P(),
            P(),
            P(),
            P(cells, None),
            P(cells, None),
        ),
        out_specs=P(rows, cells),
        check_vma=False,
    )
```

```python
import functools

import jax
import jax.numpy as jnp
from jax import lax
from jax.experimental import pallas as pl
from jax.experimental.pallas import tpu as pltpu
from jax.sharding import Mesh, PartitionSpec as P

BAND = 3
TAPS = 2 * BAND + 1
TABLES = 4
GROUP = 8
AHEAD = 3
F32 = jnp.float32
BF16 = jnp.bfloat16
VMEM = pl.BlockSpec(memory_space=pltpu.VMEM)
SMEM = pl.BlockSpec(memory_space=pltpu.SMEM)
HBM = pl.BlockSpec(memory_space=pltpu.HBM)


def split_table(table):
    high = table.astype(BF16)
    low = (table - high.astype(F32)).astype(BF16)
    return high, low


def band_column(table, tap):
    rows = lax.broadcasted_iota(jnp.int32, table.shape, 0)
    cols = lax.broadcasted_iota(jnp.int32, table.shape, 1)
    return jnp.sum(jnp.where(cols == rows + (tap - BAND), table, 0.0), axis=1, keepdims=True)


def zy_kernel(jac, table_y, table_z, index_y, index_z, out, planes, coef, lhs, done, ty, tz, iy, iz, sems, outs, small):
    slab, _, rows, ny = planes.shape
    nz = done.shape[0]
    per = nz // GROUP
    steps = slab // 2 * per
    loads = [
        pltpu.make_async_copy(s, d, small.at[k])
        for k, (s, d) in enumerate(((table_z, tz), (index_z, iz), (table_y, ty), (index_y, iy)))
    ]
    for load in loads:
        load.start()

    def wave(step):
        pair, group = step // per, step % per
        for k in range(GROUP):
            for x in range(2):
                w = group * GROUP + k
                yield pltpu.make_async_copy(
                    jac.at[:, pair * 2 + x, w, :], planes.at[pair * 2 + x, w + BAND], sems.at[pair * 2 + x, w]
                )

    def result(step):
        pair, group = step // per, step % per
        place = (pl.ds(group * GROUP, GROUP), slice(None), pl.ds(pair * 2 * rows, 2 * rows))
        return pltpu.make_async_copy(done.at[place], out.at[place], outs.at[step])

    for step in range(AHEAD):
        for copy in wave(step):
            copy.start()
    for x in range(slab):
        for edge in range(BAND):
            planes[x, edge] = jnp.zeros((rows, ny), F32)
            planes[x, nz + BAND + edge] = jnp.zeros((rows, ny), F32)
    loads[0].wait()
    loads[1].wait()
    for tap in range(TAPS):
        cols = [band_column(tz[t], tap) for t in range(TABLES)]
        for x in range(slab):
            label = iz[pl.ds(x, 1), :]
            picked = jnp.broadcast_to(cols[0], (nz, ny))
            for t in range(1, TABLES):
                picked = jnp.where(label == t, cols[t], picked)
            coef[x, tap] = picked
    loads[2].wait()
    loads[3].wait()
    split = [split_table(ty[t]) for t in range(TABLES)]
    for t in range(TABLES):
        for u in range(TABLES):
            pieces = [split[t][0], split[u][0], split[t][1], split[u][1]]
            lhs[t * TABLES + u] = jnp.concatenate(pieces, axis=1)
    half = rows // 2
    for copy in wave(0):
        copy.wait()

    for step in range(steps):
        x0, group = step // per * 2, step % per

        if step + AHEAD < steps:
            for copy in wave(step + AHEAD):
                copy.start()
        if step + 1 < steps:
            for copy in wave(step + 1):
                copy.wait()

        parts = {}
        for x in range(2):
            for h in range(2):
                use = pl.ds(h * half, half)
                for k0 in range(0, GROUP, 2):
                    held = [planes[x0 + x, group * GROUP + k0 + j, use, :] for j in range(TAPS + 1)]
                    for k in range(2):
                        z = group * GROUP + k0 + k
                        total = coef[x0 + x, 0, pl.ds(z, 1), :] * held[k]
                        for tap in range(1, TAPS):
                            total = total + coef[x0 + x, tap, pl.ds(z, 1), :] * held[k + tap]
                        short = total.astype(BF16)
                        blank = jnp.zeros_like(short)
                        parts[k0 + k, x, h] = jnp.concatenate([blank, short] if x else [short, blank], axis=1)
        for k in range(GROUP):
            z = group * GROUP + k
            rhs = jnp.concatenate([parts[k, x, h] for x in range(2) for h in range(2)], axis=0)
            both = lax.dot_general(
                lhs[iy[x0, z] * TABLES + iy[x0 + 1, z]],
                jnp.concatenate([rhs, rhs], axis=1),
                (((1,), (1,)), ((), ())),
                preferred_element_type=F32,
            )
            done[z, :, pl.ds(x0 * rows, 2 * rows)] = both.astype(BF16)
        result(step).start()

    for step in range(steps):
        result(step).wait()


def smooth_zy(jacobian, smooth_y, smooth_z, index_y, index_z):
    rows, slab, ny, nz = jacobian.shape
    return pl.pallas_call(
        zy_kernel,
        out_shape=jax.ShapeDtypeStruct((nz, ny, slab * rows), BF16),
        in_specs=[HBM] * 5,
        out_specs=HBM,
        scratch_shapes=[
            pltpu.VMEM((slab, nz + 2 * BAND, rows, ny), F32),
            pltpu.VMEM((slab, TAPS, nz, ny), F32),
            pltpu.VMEM((TABLES * TABLES, ny, 4 * ny), BF16),
            pltpu.VMEM((nz, ny, slab * rows), BF16),
            pltpu.VMEM(smooth_y.shape, F32),
            pltpu.VMEM(smooth_z.shape, F32),
            pltpu.SMEM(index_y.shape, jnp.int32),
            pltpu.VMEM(index_z.shape, jnp.int32),
            pltpu.SemaphoreType.DMA((slab, nz)),
            pltpu.SemaphoreType.DMA((slab // 2 * nz // GROUP,)),
            pltpu.SemaphoreType.DMA((4,)),
        ],
        compiler_params=pltpu.CompilerParams(vmem_limit_bytes=60 * 2**20),
        name="smooth_zy",
    )(jnp.swapaxes(jacobian, 2, 3), smooth_y, smooth_z, index_y, index_z)


def coef_kernel(place, index_x, table_x, out, bands):
    z, y0 = place[0], place[1]
    nx = table_x.shape[1]
    _, columns, lanes = out.shape
    for t in range(TABLES):
        for tap in range(TAPS):
            bands[t, tap] = jnp.broadcast_to(band_column(table_x[t], tap), (nx, lanes))
    row = index_x[pl.ds(z, 1), :]
    sub = lax.broadcasted_iota(jnp.int32, (columns, row.shape[1]), 0)
    lan = lax.broadcasted_iota(jnp.int32, (columns, row.shape[1]), 1)
    label = jnp.sum(jnp.where(lan == sub + y0, row, 0).astype(F32), axis=1, keepdims=True)
    label = jnp.broadcast_to(label, (columns, lanes))

    lane = lax.broadcasted_iota(jnp.int32, label.shape, 1)

    @pl.loop(0, out.shape[0])
    def _(cell):
        total = jnp.zeros(label.shape, F32)
        for k in range(4):
            for tap in range(TAPS):
                row = pl.ds(cell * 4 + k, 1)
                picked = jnp.broadcast_to(bands[0, tap, row, :], label.shape)
                for t in range(1, TABLES):
                    picked = jnp.where(label == t, bands[t, tap, row, :], picked)
                total = jnp.where(lane == k * TAPS + tap, picked, total)
        out[cell] = total


def x_coefs(place, index_x, smooth_x):
    nx = smooth_x.shape[1]
    return pl.pallas_call(
        coef_kernel,
        out_shape=jax.ShapeDtypeStruct((nx // 4, 16, 128), F32),
        in_specs=[SMEM, VMEM, VMEM],
        out_specs=VMEM,
        scratch_shapes=[pltpu.VMEM((TABLES, TAPS, nx, 128), F32)],
        compiler_params=pltpu.CompilerParams(vmem_limit_bytes=12 * 2**20),
        cost_estimate=pl.CostEstimate(flops=4 * 2**20, bytes_accessed=4 * 2**20, transcendentals=0),
        name="x_coefs",
    )(place, jnp.swapaxes(index_x, 0, 1), smooth_x)


def x_kernel(parity, coef, got, out, wide):
    nx, columns, lanes = out.shape
    left = lax.broadcasted_iota(jnp.int32, (columns, 128), 1) < 64
    for edge in range(BAND):
        wide[edge] = jnp.zeros(wide.shape[1:], F32)
        wide[nx + BAND + edge] = jnp.zeros(wide.shape[1:], F32)

    def merge(cell, carry):
        for zh in range(2):
            first = zh * 64 + cell // 4 * 16 + parity * 4 + cell % 4
            use = pl.ds(zh * 128, 128)
            for pair in range(2):
                a = got[first, :, pl.ds(pair * 128, 128)].astype(F32)
                b = got[first + 8, :, pl.ds(pair * 128, 128)].astype(F32)
                base = cell * 4 + pair * 2 + BAND
                wide[base, :, use] = jnp.where(left, a, pltpu.roll(b, 64, 1))
                wide[base + 1, :, use] = jnp.where(left, pltpu.roll(a, 64, 1), b)
        return carry

    def smooth(cell, carry):
        taps = coef[cell]
        for k in range(4):
            x = cell * 4 + k
            totals = [None] * (lanes // 128)
            for tap in range(TAPS):
                column = k * TAPS + tap
                factor = jnp.broadcast_to(taps[:, column : column + 1], (columns, 128))
                for block in range(lanes // 128):
                    term = factor * wide[x + tap, :, pl.ds(block * 128, 128)]
                    totals[block] = term if tap == 0 else totals[block] + term
            for block in range(lanes // 128):
                out[x, :, pl.ds(block * 128, 128)] = totals[block].astype(BF16)
        return carry

    lax.fori_loop(0, nx // 4, merge, 0, unroll=16)
    lax.fori_loop(0, nx // 4, smooth, 0, unroll=16)


def smooth_x_local(parity, coef, got):
    nx, columns = coef.shape[0] * 4, coef.shape[1]
    return pl.pallas_call(
        functools.partial(x_kernel, parity),
        out_shape=jax.ShapeDtypeStruct((nx, columns, 256), BF16),
        in_specs=[VMEM, VMEM],
        out_specs=VMEM,
        scratch_shapes=[pltpu.VMEM((nx + 2 * BAND, columns, 256), F32)],
        compiler_params=pltpu.CompilerParams(vmem_limit_bytes=12 * 2**20),
        name="smooth_x",
    )(coef, got)


def add_up(parts):
    while len(parts) > 1:
        parts = [a + b for a, b in zip(parts[::2], parts[1::2])] + parts[len(parts) // 2 * 2 :]
    return parts[0]


def gram_kernel(core, even, odd, right_even, right_odd, *rest):
    out = rest[-1]
    which = core[0]
    for x2, left in enumerate((even, odd)):
        for y2, right in enumerate((right_even, right_odd)):
            piece = lax.dot_general(
                left[...], right[...], (((0,), (0,)), ((), ())), preferred_element_type=F32
            ).astype(BF16)
            for x4 in range(2):
                for zh in range(2):
                    start = (zh * 2 + x4) * 64
                    out[x4 * 2 + x2, y2 * 2 + which, pl.ds(zh * 64, 64), :] = piece[start : start + 64]


def gram(core, left, right, *held):
    return pl.pallas_call(
        gram_kernel,
        out_shape=jax.ShapeDtypeStruct((4, 4, 128, 256), BF16),
        in_specs=[SMEM] + [VMEM] * (4 + len(held)),
        out_specs=VMEM,
        input_output_aliases={5: 0} if held else {},
        compiler_params=pltpu.CompilerParams(vmem_limit_bytes=16 * 2**20),
        cost_estimate=pl.CostEstimate(flops=2**29, bytes_accessed=2**21, transcendentals=0),
        name="gram",
    )(core, *left, *right, *held)


def sum_plane_kernel(got, out):
    for zh in range(2):
        for pair in range(2):
            rows, lanes = pl.ds(zh * 64, 64), pl.ds(pair * 128, 128)
            total = add_up([got[k, rows, lanes].astype(F32) for k in range(got.shape[0])])
            left = lax.broadcasted_iota(jnp.int32, (32, 128), 1) < 64
            upper, lower = total[:32], total[32:]
            out[zh * 4 + pair * 2] = jnp.where(left, upper, pltpu.roll(lower, 64, 1))
            out[zh * 4 + pair * 2 + 1] = jnp.where(left, pltpu.roll(upper, 64, 1), lower)


def sum_plane(got):
    return pl.pallas_call(
        sum_plane_kernel,
        out_shape=jax.ShapeDtypeStruct((8, 32, 128), F32),
        in_specs=[VMEM],
        out_specs=VMEM,
        compiler_params=pltpu.CompilerParams(vmem_limit_bytes=8 * 2**20),
        name="sum_plane",
    )(got)


def sum_line_kernel(got, out):
    total = add_up([got[k] for k in range(got.shape[0])])
    out[pl.ds(0, 32), :] = total[:, :64]
    out[pl.ds(32, 32), :] = total[:, 64:]


def sum_line(got):
    return pl.pallas_call(
        sum_line_kernel,
        out_shape=jax.ShapeDtypeStruct((64, 64), F32),
        in_specs=[VMEM],
        out_specs=VMEM,
        compiler_params=pltpu.CompilerParams(vmem_limit_bytes=4 * 2**20),
        name="sum_line",
    )(got)


def body(jacobian, smooth_x, smooth_y, smooth_z, index_x, index_y, index_z):
    sent = smooth_zy(jacobian, smooth_y, smooth_z, index_y, index_z)
    nz, ny, width = sent.shape
    place = jnp.stack([lax.axis_index(("zh", "zl", "x")), lax.axis_index("y") * 16]).astype(jnp.int32)
    coef = x_coefs(place, index_x, smooth_x)
    got = lax.all_to_all(
        sent.reshape(128, nz * ny // 128, width), ("zh", "zl", "x", "y"), 0, 0, tiled=True
    )
    core = lax.axis_index("core").reshape(1).astype(jnp.int32)
    own, other = [], []
    for parity in range(2):
        own.append(smooth_x_local(parity, coef, got).reshape(-1, 256))
        other.append(lax.ppermute(own[parity], "core", [(0, 1), (1, 0)]))
    partial = gram(1 - core, own, other, gram(core, own, own))
    plane = lax.all_to_all(partial.reshape(16, 128, 256), ("x", "y"), 0, 0, tiled=True)
    line = lax.all_to_all(sum_plane(plane), ("zh", "zl"), 0, 0, tiled=True)
    return sum_line(line)


def solution(mesh):
    fine = Mesh(mesh.devices.reshape(2, 4, 2, 4, 4), ("zh", "x", "core", "zl", "y"))
    rows, cells = ("zh", "x", "core"), ("zl", "y")
    return jax.shard_map(
        body,
        mesh=fine,
        in_specs=(
            P(rows, cells, None, None),
            P(),
            P(),
            P(),
            P(),
            P(cells, None),
            P(cells, None),
        ),
        out_specs=P(rows, cells),
        check_vma=False,
    )
```

```python
import jax
import jax.numpy as jnp
from jax import lax
from jax.experimental import pallas as pl
from jax.experimental.pallas import tpu as pltpu
from jax.sharding import Mesh, PartitionSpec as P

BAND = 3
TAPS = 2 * BAND + 1
TABLES = 4
GROUP = 8
AHEAD = 3
F32 = jnp.float32
BF16 = jnp.bfloat16
VMEM = pl.BlockSpec(memory_space=pltpu.VMEM)
SMEM = pl.BlockSpec(memory_space=pltpu.SMEM)
HBM = pl.BlockSpec(memory_space=pltpu.HBM)


def split_table(table):
    high = table.astype(BF16)
    low = (table - high.astype(F32)).astype(BF16)
    return high, low


def band_column(table, tap):
    rows = lax.broadcasted_iota(jnp.int32, table.shape, 0)
    cols = lax.broadcasted_iota(jnp.int32, table.shape, 1)
    return jnp.sum(jnp.where(cols == rows + (tap - BAND), table, 0.0), axis=1, keepdims=True)


def zy_kernel(jac, table_y, table_z, index_y, index_z, out, planes, coef, lhs, done, ty, tz, iy, iz, sems, outs, small):
    slab, _, rows, ny = planes.shape
    nz = done.shape[0]
    per = nz // GROUP
    steps = slab // 2 * per
    loads = [
        pltpu.make_async_copy(s, d, small.at[k])
        for k, (s, d) in enumerate(((table_z, tz), (index_z, iz), (table_y, ty), (index_y, iy)))
    ]
    for load in loads:
        load.start()

    def wave(step):
        pair, group = step // per, step % per
        for k in range(GROUP):
            for x in range(2):
                w = group * GROUP + k
                yield pltpu.make_async_copy(
                    jac.at[:, pair * 2 + x, w, :], planes.at[pair * 2 + x, w + BAND], sems.at[step]
                )

    def arrived(step):
        pair, group = step // per, step % per
        whole = planes.at[pl.ds(pair * 2, 2), pl.ds(group * GROUP + BAND, GROUP)]
        pltpu.make_async_copy(whole, whole, sems.at[step]).wait()

    def result(step):
        pair, group = step // per, step % per
        place = (pl.ds(group * GROUP, GROUP), slice(None), pl.ds(pair * 2 * rows, 2 * rows))
        return pltpu.make_async_copy(done.at[place], out.at[place], outs)

    for step in range(AHEAD):
        for copy in wave(step):
            copy.start()
    for x in range(slab):
        for edge in range(BAND):
            planes[x, edge] = jnp.zeros((rows, ny), F32)
            planes[x, nz + BAND + edge] = jnp.zeros((rows, ny), F32)
    loads[0].wait()
    loads[1].wait()
    for tap in range(TAPS):
        cols = [band_column(tz[t], tap) for t in range(TABLES)]
        for x in range(slab):
            label = iz[pl.ds(x, 1), :]
            picked = jnp.broadcast_to(cols[0], (nz, ny))
            for t in range(1, TABLES):
                picked = jnp.where(label == t, cols[t], picked)
            coef[x, tap] = picked
    loads[2].wait()
    loads[3].wait()
    split = [split_table(ty[t]) for t in range(TABLES)]
    for t in range(TABLES):
        for u in range(TABLES):
            pieces = [split[t][0], split[u][0], split[t][1], split[u][1]]
            lhs[t * TABLES + u] = jnp.concatenate(pieces, axis=1)
    half = rows // 2
    arrived(0)

    for step in range(steps):
        x0, group = step // per * 2, step % per

        if step + AHEAD < steps:
            for copy in wave(step + AHEAD):
                copy.start()
        if step + 1 < steps:
            arrived(step + 1)

        parts = {}
        for x in range(2):
            for h in range(2):
                use = pl.ds(h * half, half)
                for k0 in range(0, GROUP, 2):
                    held = [planes[x0 + x, group * GROUP + k0 + j, use, :] for j in range(TAPS + 1)]
                    for k in range(2):
                        z = group * GROUP + k0 + k
                        total = coef[x0 + x, 0, pl.ds(z, 1), :] * held[k]
                        for tap in range(1, TAPS):
                            total = total + coef[x0 + x, tap, pl.ds(z, 1), :] * held[k + tap]
                        short = total.astype(BF16)
                        blank = jnp.zeros_like(short)
                        parts[k0 + k, x, h] = jnp.concatenate([blank, short] if x else [short, blank], axis=1)
        for k in range(GROUP):
            z = group * GROUP + k
            rhs = jnp.concatenate([parts[k, x, h] for x in range(2) for h in range(2)], axis=0)
            both = lax.dot_general(
                lhs[iy[x0, z] * TABLES + iy[x0 + 1, z]],
                jnp.concatenate([rhs, rhs], axis=1),
                (((1,), (1,)), ((), ())),
                preferred_element_type=F32,
            )
            done[z, :, pl.ds(x0 * rows, 2 * rows)] = both.astype(BF16)
        result(step).start()

    pltpu.make_async_copy(done, out, outs).wait()


def smooth_zy(jacobian, smooth_y, smooth_z, index_y, index_z):
    rows, slab, ny, nz = jacobian.shape
    return pl.pallas_call(
        zy_kernel,
        out_shape=jax.ShapeDtypeStruct((nz, ny, slab * rows), BF16),
        in_specs=[HBM] * 5,
        out_specs=HBM,
        scratch_shapes=[
            pltpu.VMEM((slab, nz + 2 * BAND, rows, ny), F32),
            pltpu.VMEM((slab, TAPS, nz, ny), F32),
            pltpu.VMEM((TABLES * TABLES, ny, 4 * ny), BF16),
            pltpu.VMEM((nz, ny, slab * rows), BF16),
            pltpu.VMEM(smooth_y.shape, F32),
            pltpu.VMEM(smooth_z.shape, F32),
            pltpu.SMEM(index_y.shape, jnp.int32),
            pltpu.VMEM(index_z.shape, jnp.int32),
            pltpu.SemaphoreType.DMA((slab // 2 * nz // GROUP,)),
            pltpu.SemaphoreType.DMA,
            pltpu.SemaphoreType.DMA((4,)),
        ],
        compiler_params=pltpu.CompilerParams(vmem_limit_bytes=60 * 2**20),
        name="smooth_zy",
    )(jnp.swapaxes(jacobian, 2, 3), smooth_y, smooth_z, index_y, index_z)


def coef_kernel(place, index_x, table_x, out, bands):
    z, y0 = place[0], place[1]
    nx = table_x.shape[1]
    _, columns, lanes = out.shape
    for t in range(TABLES):
        for tap in range(TAPS):
            bands[t, tap] = jnp.broadcast_to(band_column(table_x[t], tap), (nx, lanes))
    row = index_x[pl.ds(z, 1), :]
    sub = lax.broadcasted_iota(jnp.int32, (columns, row.shape[1]), 0)
    lan = lax.broadcasted_iota(jnp.int32, (columns, row.shape[1]), 1)
    label = jnp.sum(jnp.where(lan == sub + y0, row, 0).astype(F32), axis=1, keepdims=True)
    label = jnp.broadcast_to(label, (columns, lanes))

    lane = lax.broadcasted_iota(jnp.int32, label.shape, 1)

    @pl.loop(0, out.shape[0])
    def _(cell):
        total = jnp.zeros(label.shape, F32)
        for k in range(4):
            for tap in range(TAPS):
                row = pl.ds(cell * 4 + k, 1)
                picked = jnp.broadcast_to(bands[0, tap, row, :], label.shape)
                for t in range(1, TABLES):
                    picked = jnp.where(label == t, bands[t, tap, row, :], picked)
                total = jnp.where(lane == k * TAPS + tap, picked, total)
        out[cell] = total


def x_coefs(place, index_x, smooth_x):
    nx = smooth_x.shape[1]
    return pl.pallas_call(
        coef_kernel,
        out_shape=jax.ShapeDtypeStruct((nx // 4, 16, 128), F32),
        in_specs=[SMEM, VMEM, VMEM],
        out_specs=VMEM,
        scratch_shapes=[pltpu.VMEM((TABLES, TAPS, nx, 128), F32)],
        compiler_params=pltpu.CompilerParams(vmem_limit_bytes=12 * 2**20),
        cost_estimate=pl.CostEstimate(flops=4 * 2**20, bytes_accessed=4 * 2**20, transcendentals=0),
        name="x_coefs",
    )(place, jnp.swapaxes(index_x, 0, 1), smooth_x)


def x_kernel(coef, got, out, wide):
    nx, columns, lanes = out.shape
    left = lax.broadcasted_iota(jnp.int32, (columns, 128), 1) < 64
    for edge in range(BAND):
        wide[edge] = jnp.zeros(wide.shape[1:], F32)
        wide[nx + BAND + edge] = jnp.zeros(wide.shape[1:], F32)

    def merge(cell, carry):
        for parity in range(2):
            for zh in range(2):
                first = zh * 64 + cell // 4 * 16 + parity * 4 + cell % 4
                use = pl.ds((parity * 2 + zh) * 128, 128)
                for pair in range(2):
                    a = got[first, :, pl.ds(pair * 128, 128)].astype(F32)
                    b = got[first + 8, :, pl.ds(pair * 128, 128)].astype(F32)
                    base = cell * 4 + pair * 2 + BAND
                    wide[base, :, use] = jnp.where(left, a, pltpu.roll(b, 64, 1))
                    wide[base + 1, :, use] = jnp.where(left, pltpu.roll(a, 64, 1), b)
        return carry

    def smooth(cell, carry):
        taps = coef[cell]
        for k in range(4):
            x = cell * 4 + k
            totals = [None] * (lanes // 128)
            for tap in range(TAPS):
                column = k * TAPS + tap
                factor = jnp.broadcast_to(taps[:, column : column + 1], (columns, 128))
                for block in range(lanes // 128):
                    term = factor * wide[x + tap, :, pl.ds(block * 128, 128)]
                    totals[block] = term if tap == 0 else totals[block] + term
            for block in range(lanes // 128):
                out[x, :, pl.ds(block * 128, 128)] = totals[block].astype(BF16)
        return carry

    lax.fori_loop(0, nx // 4, merge, 0, unroll=16)
    lax.fori_loop(0, nx // 4, smooth, 0, unroll=16)


def smooth_x_local(coef, got):
    nx, columns = coef.shape[0] * 4, coef.shape[1]
    return pl.pallas_call(
        x_kernel,
        out_shape=jax.ShapeDtypeStruct((nx, columns, 512), BF16),
        in_specs=[VMEM, VMEM],
        out_specs=VMEM,
        scratch_shapes=[pltpu.VMEM((nx + 2 * BAND, columns, 512), F32)],
        compiler_params=pltpu.CompilerParams(vmem_limit_bytes=12 * 2**20),
        name="smooth_x",
    )(coef, got)


def add_up(parts):
    while len(parts) > 1:
        parts = [a + b for a, b in zip(parts[::2], parts[1::2])] + parts[len(parts) // 2 * 2 :]
    return parts[0]


def gram_kernel(core, own, right, *rest):
    out = rest[-1]
    which = core[0]
    left = own[...]
    for part in range(2):
        piece = lax.dot_general(
            left,
            right[:, part * 256 : (part + 1) * 256],
            (((0,), (0,)), ((), ())),
            preferred_element_type=F32,
        ).astype(BF16)
        for x in range(4):
            for zh in range(2):
                start = ((x % 2 * 2 + zh) * 2 + x // 2) * 64
                out[x, part * 2 + which, pl.ds(zh * 64, 64), :] = piece[start : start + 64]


def gram(core, own, right, *held):
    return pl.pallas_call(
        gram_kernel,
        out_shape=jax.ShapeDtypeStruct((4, 4, 128, 256), BF16),
        in_specs=[SMEM] + [VMEM] * (2 + len(held)),
        out_specs=VMEM,
        input_output_aliases={3: 0} if held else {},
        compiler_params=pltpu.CompilerParams(vmem_limit_bytes=16 * 2**20),
        cost_estimate=pl.CostEstimate(flops=2**29, bytes_accessed=2**21, transcendentals=0),
        name="gram",
    )(core, own, right, *held)


def sum_plane_kernel(got, out):
    for zh in range(2):
        for pair in range(2):
            rows, lanes = pl.ds(zh * 64, 64), pl.ds(pair * 128, 128)
            total = add_up([got[k, rows, lanes].astype(F32) for k in range(got.shape[0])])
            left = lax.broadcasted_iota(jnp.int32, (32, 128), 1) < 64
            upper, lower = total[:32], total[32:]
            out[zh * 4 + pair * 2] = jnp.where(left, upper, pltpu.roll(lower, 64, 1))
            out[zh * 4 + pair * 2 + 1] = jnp.where(left, pltpu.roll(upper, 64, 1), lower)


def sum_plane(got):
    return pl.pallas_call(
        sum_plane_kernel,
        out_shape=jax.ShapeDtypeStruct((8, 32, 128), F32),
        in_specs=[VMEM],
        out_specs=VMEM,
        compiler_params=pltpu.CompilerParams(vmem_limit_bytes=8 * 2**20),
        name="sum_plane",
    )(got)


def sum_line_kernel(got, out):
    total = add_up([got[k] for k in range(got.shape[0])])
    out[pl.ds(0, 32), :] = total[:, :64]
    out[pl.ds(32, 32), :] = total[:, 64:]


def sum_line(got):
    return pl.pallas_call(
        sum_line_kernel,
        out_shape=jax.ShapeDtypeStruct((64, 64), F32),
        in_specs=[VMEM],
        out_specs=VMEM,
        compiler_params=pltpu.CompilerParams(vmem_limit_bytes=4 * 2**20),
        name="sum_line",
    )(got)


def body(jacobian, smooth_x, smooth_y, smooth_z, index_x, index_y, index_z):
    sent = smooth_zy(jacobian, smooth_y, smooth_z, index_y, index_z)
    nz, ny, width = sent.shape
    place = jnp.stack([lax.axis_index(("zh", "zl", "x")), lax.axis_index("y") * 16]).astype(jnp.int32)
    coef = x_coefs(place, index_x, smooth_x)
    got = lax.all_to_all(
        sent.reshape(128, nz * ny // 128, width), ("zh", "zl", "x", "y"), 0, 0, tiled=True
    )
    panel = smooth_x_local(coef, got)
    own = panel.reshape(-1, panel.shape[2])
    other = lax.ppermute(own, "core", [(0, 1), (1, 0)])
    core = lax.axis_index("core").reshape(1).astype(jnp.int32)
    partial = gram(1 - core, own, other, gram(core, own, own))
    plane = lax.all_to_all(partial.reshape(16, 128, 256), ("x", "y"), 0, 0, tiled=True)
    line = lax.all_to_all(sum_plane(plane), ("zh", "zl"), 0, 0, tiled=True)
    return sum_line(line)


def solution(mesh):
    fine = Mesh(mesh.devices.reshape(2, 4, 2, 4, 4), ("zh", "x", "core", "zl", "y"))
    rows, cells = ("zh", "x", "core"), ("zl", "y")
    return jax.shard_map(
        body,
        mesh=fine,
        in_specs=(
            P(rows, cells, None, None),
            P(),
            P(),
            P(),
            P(),
            P(cells, None),
            P(cells, None),
        ),
        out_specs=P(rows, cells),
        check_vma=False,
    )
```

```python
import functools

import jax
import jax.numpy as jnp
from jax import lax
from jax.experimental import pallas as pl
from jax.experimental.pallas import tpu as pltpu
from jax.sharding import Mesh, PartitionSpec as P

BAND = 3
TAPS = 2 * BAND + 1
TABLES = 4
GROUP = 8
AHEAD = 4
F32 = jnp.float32
BF16 = jnp.bfloat16
VMEM = pl.BlockSpec(memory_space=pltpu.VMEM)
SMEM = pl.BlockSpec(memory_space=pltpu.SMEM)
HBM = pl.BlockSpec(memory_space=pltpu.HBM)


def split_table(table):
    high = table.astype(BF16)
    low = (table - high.astype(F32)).astype(BF16)
    return high, low


def band_column(table, tap):
    rows = lax.broadcasted_iota(jnp.int32, table.shape, 0)
    cols = lax.broadcasted_iota(jnp.int32, table.shape, 1)
    return jnp.sum(jnp.where(cols == rows + (tap - BAND), table, 0.0), axis=1, keepdims=True)


def zy_kernel(jac, table_y, table_z, index_y, index_z, out, planes, coef, lhs, done, ty, tz, iy, iz, sems, outs, small):
    slab, _, rows, ny = planes.shape
    nz = done.shape[0]
    per = nz // GROUP
    steps = slab // 2 * per
    loads = [
        pltpu.make_async_copy(s, d, small.at[k])
        for k, (s, d) in enumerate(((table_z, tz), (index_z, iz), (table_y, ty), (index_y, iy)))
    ]
    for load in loads:
        load.start()

    def wave(step):
        pair, group = step // per, step % per
        for k in range(GROUP):
            for x in range(2):
                w = group * GROUP + k
                yield pltpu.make_async_copy(
                    jac.at[:, pair * 2 + x, w, :], planes.at[pair * 2 + x, w + BAND], sems.at[step]
                )

    def arrived(step):
        pair, group = step // per, step % per
        whole = planes.at[pl.ds(pair * 2, 2), pl.ds(group * GROUP + BAND, GROUP)]
        pltpu.make_async_copy(whole, whole, sems.at[step]).wait()

    def result(step):
        pair, group = step // per, step % per
        place = (pl.ds(group * GROUP, GROUP), slice(None), pl.ds(pair * 2 * rows, 2 * rows))
        return pltpu.make_async_copy(done.at[place], out.at[place], outs)

    for step in range(AHEAD):
        for k, copy in enumerate(wave(step)):
            copy.start(priority=k % 2)
    for x in range(slab):
        for edge in range(BAND):
            planes[x, edge] = jnp.zeros((rows, ny), F32)
            planes[x, nz + BAND + edge] = jnp.zeros((rows, ny), F32)
    loads[0].wait()
    loads[1].wait()
    for tap in range(TAPS):
        cols = [band_column(tz[t], tap) for t in range(TABLES)]
        for x in range(slab):
            label = iz[pl.ds(x, 1), :]
            picked = jnp.broadcast_to(cols[0], (nz, ny))
            for t in range(1, TABLES):
                picked = jnp.where(label == t, cols[t], picked)
            coef[x, tap] = picked
    loads[2].wait()
    loads[3].wait()
    split = [split_table(ty[t]) for t in range(TABLES)]
    for t in range(TABLES):
        for u in range(TABLES):
            pieces = [split[t][0], split[u][0], split[t][1], split[u][1]]
            lhs[t * TABLES + u] = jnp.concatenate(pieces, axis=1)
    half = rows // 2
    arrived(0)

    for step in range(steps):
        x0, group = step // per * 2, step % per

        if step + AHEAD < steps:
            for k, copy in enumerate(wave(step + AHEAD)):
                copy.start(priority=k % 2)
        if step + 1 < steps:
            arrived(step + 1)

        parts = {}
        for x in range(2):
            for h in range(2):
                use = pl.ds(h * half, half)
                for k0 in range(0, GROUP, 2):
                    held = [planes[x0 + x, group * GROUP + k0 + j, use, :] for j in range(TAPS + 1)]
                    for k in range(2):
                        z = group * GROUP + k0 + k
                        total = coef[x0 + x, 0, pl.ds(z, 1), :] * held[k]
                        for tap in range(1, TAPS):
                            total = total + coef[x0 + x, tap, pl.ds(z, 1), :] * held[k + tap]
                        short = total.astype(BF16)
                        blank = jnp.zeros_like(short)
                        parts[k0 + k, x, h] = jnp.concatenate([blank, short] if x else [short, blank], axis=1)
        for k in range(GROUP):
            z = group * GROUP + k
            rhs = jnp.concatenate([parts[k, x, h] for x in range(2) for h in range(2)], axis=0)
            both = lax.dot_general(
                lhs[iy[x0, z] * TABLES + iy[x0 + 1, z]],
                jnp.concatenate([rhs, rhs], axis=1),
                (((1,), (1,)), ((), ())),
                preferred_element_type=F32,
            )
            done[z, :, pl.ds(x0 * rows, 2 * rows)] = both.astype(BF16)
        result(step).start()

    pltpu.make_async_copy(done, out, outs).wait()


def smooth_zy(jacobian, smooth_y, smooth_z, index_y, index_z):
    rows, slab, ny, nz = jacobian.shape
    return pl.pallas_call(
        zy_kernel,
        out_shape=jax.ShapeDtypeStruct((nz, ny, slab * rows), BF16),
        in_specs=[HBM] * 5,
        out_specs=HBM,
        scratch_shapes=[
            pltpu.VMEM((slab, nz + 2 * BAND, rows, ny), F32),
            pltpu.VMEM((slab, TAPS, nz, ny), F32),
            pltpu.VMEM((TABLES * TABLES, ny, 4 * ny), BF16),
            pltpu.VMEM((nz, ny, slab * rows), BF16),
            pltpu.VMEM(smooth_y.shape, F32),
            pltpu.VMEM(smooth_z.shape, F32),
            pltpu.SMEM(index_y.shape, jnp.int32),
            pltpu.VMEM(index_z.shape, jnp.int32),
            pltpu.SemaphoreType.DMA((slab // 2 * nz // GROUP,)),
            pltpu.SemaphoreType.DMA,
            pltpu.SemaphoreType.DMA((4,)),
        ],
        compiler_params=pltpu.CompilerParams(vmem_limit_bytes=60 * 2**20),
        name="smooth_zy",
    )(jnp.swapaxes(jacobian, 2, 3), smooth_y, smooth_z, index_y, index_z)


def coef_kernel(place, index_x, table_x, out, bands):
    z, y0 = place[0], place[1]
    nx = table_x.shape[1]
    _, columns, lanes = out.shape
    for t in range(TABLES):
        for tap in range(TAPS):
            bands[t, tap] = jnp.broadcast_to(band_column(table_x[t], tap), (nx, lanes))
    row = index_x[pl.ds(z, 1), :]
    sub = lax.broadcasted_iota(jnp.int32, (columns, row.shape[1]), 0)
    lan = lax.broadcasted_iota(jnp.int32, (columns, row.shape[1]), 1)
    label = jnp.sum(jnp.where(lan == sub + y0, row, 0).astype(F32), axis=1, keepdims=True)
    label = jnp.broadcast_to(label, (columns, lanes))

    lane = lax.broadcasted_iota(jnp.int32, label.shape, 1)

    @pl.loop(0, out.shape[0])
    def _(cell):
        total = jnp.zeros(label.shape, F32)
        for k in range(4):
            for tap in range(TAPS):
                row = pl.ds(cell * 4 + k, 1)
                picked = jnp.broadcast_to(bands[0, tap, row, :], label.shape)
                for t in range(1, TABLES):
                    picked = jnp.where(label == t, bands[t, tap, row, :], picked)
                total = jnp.where(lane == k * TAPS + tap, picked, total)
        out[cell] = total


def x_coefs(place, index_x, smooth_x):
    nx = smooth_x.shape[1]
    return pl.pallas_call(
        coef_kernel,
        out_shape=jax.ShapeDtypeStruct((nx // 4, 16, 128), F32),
        in_specs=[SMEM, VMEM, VMEM],
        out_specs=VMEM,
        scratch_shapes=[pltpu.VMEM((TABLES, TAPS, nx, 128), F32)],
        compiler_params=pltpu.CompilerParams(vmem_limit_bytes=12 * 2**20),
        cost_estimate=pl.CostEstimate(flops=4 * 2**20, bytes_accessed=4 * 2**20, transcendentals=0),
        name="x_coefs",
    )(place, jnp.swapaxes(index_x, 0, 1), smooth_x)


def x_kernel(part, coef, got, out, wide):
    nx, columns, lanes = out.shape
    cells = nx // 4
    left = lax.broadcasted_iota(jnp.int32, (columns, 128), 1) < 64
    for edge in range(4):
        wide[edge + part * (nx + 4)] = jnp.zeros(wide.shape[1:], F32)

    for k in range(1 - part, cells + 2 - part):
        cell = part * cells + k - 1
        for parity in range(2):
            for zh in range(2):
                first = zh * 64 + cell // 4 * 16 + parity * 4 + cell % 4
                use = pl.ds((parity * 2 + zh) * 128, 128)
                for pair in range(2):
                    a = got[first, :, pl.ds(pair * 128, 128)].astype(F32)
                    b = got[first + 8, :, pl.ds(pair * 128, 128)].astype(F32)
                    base = k * 4 + pair * 2
                    wide[base, :, use] = jnp.where(left, a, pltpu.roll(b, 64, 1))
                    wide[base + 1, :, use] = jnp.where(left, pltpu.roll(a, 64, 1), b)

    for x in range(nx):
        taps = coef[part * cells + x // 4]
        totals = [None] * (lanes // 128)
        for tap in range(TAPS):
            column = x % 4 * TAPS + tap
            factor = jnp.broadcast_to(taps[:, column : column + 1], (columns, 128))
            for block in range(lanes // 128):
                term = factor * wide[x + tap + 4 - BAND, :, pl.ds(block * 128, 128)]
                totals[block] = term if tap == 0 else totals[block] + term
        for block in range(lanes // 128):
            out[x, :, pl.ds(block * 128, 128)] = totals[block].astype(BF16)


def smooth_x_local(part, coef, got):
    nx, columns = coef.shape[0] * 2, coef.shape[1]
    return pl.pallas_call(
        functools.partial(x_kernel, part),
        out_shape=jax.ShapeDtypeStruct((nx, columns, 512), BF16),
        in_specs=[VMEM, VMEM],
        out_specs=VMEM,
        scratch_shapes=[pltpu.VMEM((nx + 8, columns, 512), F32)],
        compiler_params=pltpu.CompilerParams(vmem_limit_bytes=12 * 2**20),
        name="smooth_x",
    )(coef, got).reshape(nx * columns, 512)


def add_up(parts):
    while len(parts) > 1:
        parts = [a + b for a, b in zip(parts[::2], parts[1::2])] + parts[len(parts) // 2 * 2 :]
    return parts[0]


def gram_kernel(core, own_a, own_b, right_a, right_b, *rest):
    out = rest[-1]
    which = core[0]
    for part in range(2):
        piece = sum(
            lax.dot_general(
                own[...],
                right[:, part * 256 : (part + 1) * 256],
                (((0,), (0,)), ((), ())),
                preferred_element_type=F32,
            )
            for own, right in ((own_a, right_a), (own_b, right_b))
        ).astype(BF16)
        for x in range(4):
            for zh in range(2):
                start = ((x % 2 * 2 + zh) * 2 + x // 2) * 64
                out[x, part * 2 + which, pl.ds(zh * 64, 64), :] = piece[start : start + 64]


def gram(core, own, right, *held):
    return pl.pallas_call(
        gram_kernel,
        out_shape=jax.ShapeDtypeStruct((4, 4, 128, 256), BF16),
        in_specs=[SMEM] + [VMEM] * (4 + len(held)),
        out_specs=VMEM,
        input_output_aliases={5: 0} if held else {},
        compiler_params=pltpu.CompilerParams(vmem_limit_bytes=16 * 2**20),
        cost_estimate=pl.CostEstimate(flops=2**29, bytes_accessed=2**21, transcendentals=0),
        name="gram",
    )(core, *own, *right, *held)


def sum_plane_kernel(got, out):
    for zh in range(2):
        for pair in range(2):
            rows, lanes = pl.ds(zh * 64, 64), pl.ds(pair * 128, 128)
            total = add_up([got[k, rows, lanes].astype(F32) for k in range(got.shape[0])])
            left = lax.broadcasted_iota(jnp.int32, (32, 128), 1) < 64
            upper, lower = total[:32], total[32:]
            out[zh * 4 + pair * 2] = jnp.where(left, upper, pltpu.roll(lower, 64, 1))
            out[zh * 4 + pair * 2 + 1] = jnp.where(left, pltpu.roll(upper, 64, 1), lower)


def sum_plane(got):
    return pl.pallas_call(
        sum_plane_kernel,
        out_shape=jax.ShapeDtypeStruct((8, 32, 128), F32),
        in_specs=[VMEM],
        out_specs=VMEM,
        compiler_params=pltpu.CompilerParams(vmem_limit_bytes=8 * 2**20),
        name="sum_plane",
    )(got)


def sum_line_kernel(got, out):
    total = add_up([got[k] for k in range(got.shape[0])])
    out[pl.ds(0, 32), :] = total[:, :64]
    out[pl.ds(32, 32), :] = total[:, 64:]


def sum_line(got):
    return pl.pallas_call(
        sum_line_kernel,
        out_shape=jax.ShapeDtypeStruct((64, 64), F32),
        in_specs=[VMEM],
        out_specs=VMEM,
        compiler_params=pltpu.CompilerParams(vmem_limit_bytes=4 * 2**20),
        name="sum_line",
    )(got)


def body(jacobian, smooth_x, smooth_y, smooth_z, index_x, index_y, index_z):
    sent = smooth_zy(jacobian, smooth_y, smooth_z, index_y, index_z)
    nz, ny, width = sent.shape
    place = jnp.stack([lax.axis_index(("zh", "zl", "x")), lax.axis_index("y") * 16]).astype(jnp.int32)
    coef = x_coefs(place, index_x, smooth_x)
    got = lax.all_to_all(
        sent.reshape(128, nz * ny // 128, width), ("zh", "zl", "x", "y"), 0, 0, tiled=True
    )
    own, other = [], []
    for part in range(2):
        own.append(smooth_x_local(part, coef, got))
        other.append(lax.ppermute(own[part], "core", [(0, 1), (1, 0)]))
    core = lax.axis_index("core").reshape(1).astype(jnp.int32)
    partial = gram(1 - core, own, other, gram(core, own, own))
    plane = lax.all_to_all(partial.reshape(16, 128, 256), ("x", "y"), 0, 0, tiled=True)
    line = lax.all_to_all(sum_plane(plane), ("zh", "zl"), 0, 0, tiled=True)
    return sum_line(line)


def solution(mesh):
    fine = Mesh(mesh.devices.reshape(2, 4, 2, 4, 4), ("zh", "x", "core", "zl", "y"))
    rows, cells = ("zh", "x", "core"), ("zl", "y")
    return jax.shard_map(
        body,
        mesh=fine,
        in_specs=(
            P(rows, cells, None, None),
            P(),
            P(),
            P(),
            P(),
            P(cells, None),
            P(cells, None),
        ),
        out_specs=P(rows, cells),
        check_vma=False,
    )
```

```python
import functools

import jax
import jax.numpy as jnp
from jax import lax
from jax.experimental import pallas as pl
from jax.experimental.pallas import tpu as pltpu
from jax.sharding import Mesh, PartitionSpec as P

BAND = 3
TAPS = 2 * BAND + 1
TABLES = 4
GROUP = 16
AHEAD = 2
F32 = jnp.float32
BF16 = jnp.bfloat16
VMEM = pl.BlockSpec(memory_space=pltpu.VMEM)
SMEM = pl.BlockSpec(memory_space=pltpu.SMEM)
HBM = pl.BlockSpec(memory_space=pltpu.HBM)


def split_table(table):
    high = table.astype(BF16)
    low = (table - high.astype(F32)).astype(BF16)
    return high, low


def band_column(table, tap):
    rows = lax.broadcasted_iota(jnp.int32, table.shape, 0)
    cols = lax.broadcasted_iota(jnp.int32, table.shape, 1)
    return jnp.sum(jnp.where(cols == rows + (tap - BAND), table, 0.0), axis=1, keepdims=True)


def zy_kernel(jac, table_y, table_z, index_y, index_z, out, planes, coef, lhs, done, ty, tz, iy, iz, sems, outs, small):
    slab, _, rows, ny = planes.shape
    nz = done.shape[0]
    per = nz // GROUP
    steps = slab // 2 * per
    loads = [
        pltpu.make_async_copy(s, d, small.at[k])
        for k, (s, d) in enumerate(((table_z, tz), (index_z, iz), (table_y, ty), (index_y, iy)))
    ]
    for load in loads:
        load.start()

    def wave(step):
        pair, group = step // per, step % per
        for k in range(GROUP):
            for x in range(2):
                w = group * GROUP + k
                yield pltpu.make_async_copy(
                    jac.at[:, pair * 2 + x, w, :], planes.at[pair * 2 + x, w + BAND], sems.at[step]
                )

    def arrived(step):
        pair, group = step // per, step % per
        whole = planes.at[pl.ds(pair * 2, 2), pl.ds(group * GROUP + BAND, GROUP)]
        pltpu.make_async_copy(whole, whole, sems.at[step]).wait()

    def result(step):
        pair, group = step // per, step % per
        place = (pl.ds(group * GROUP, GROUP), slice(None), pl.ds(pair * 2 * rows, 2 * rows))
        return pltpu.make_async_copy(done.at[place], out.at[place], outs)

    for step in range(AHEAD):
        for k, copy in enumerate(wave(step)):
            copy.start(priority=k % 2)
    for x in range(slab):
        for edge in range(BAND):
            planes[x, edge] = jnp.zeros((rows, ny), F32)
            planes[x, nz + BAND + edge] = jnp.zeros((rows, ny), F32)
    loads[0].wait()
    loads[1].wait()
    for tap in range(TAPS):
        cols = [band_column(tz[t], tap) for t in range(TABLES)]
        for x in range(slab):
            label = iz[pl.ds(x, 1), :]
            picked = jnp.broadcast_to(cols[0], (nz, ny))
            for t in range(1, TABLES):
                picked = jnp.where(label == t, cols[t], picked)
            coef[x, tap] = picked
    loads[2].wait()
    loads[3].wait()
    split = [split_table(ty[t]) for t in range(TABLES)]
    for t in range(TABLES):
        for u in range(TABLES):
            pieces = [split[t][0], split[u][0], split[t][1], split[u][1]]
            lhs[t * TABLES + u] = jnp.concatenate(pieces, axis=1)
    half = rows // 2
    arrived(0)

    for step in range(steps):
        x0, group = step // per * 2, step % per

        if step + AHEAD < steps:
            for k, copy in enumerate(wave(step + AHEAD)):
                copy.start(priority=k % 2)
        parts = {}
        for k0 in range(0, GROUP, 2):
            if k0 + BAND + 1 in (GROUP, GROUP + 1) and step + 1 < steps:
                arrived(step + 1)
            for x in range(2):
                for h in range(2):
                    use = pl.ds(h * half, half)
                    held = [planes[x0 + x, group * GROUP + k0 + j, use, :] for j in range(TAPS + 1)]
                    for k in range(2):
                        z = group * GROUP + k0 + k
                        total = coef[x0 + x, 0, pl.ds(z, 1), :] * held[k]
                        for tap in range(1, TAPS):
                            total = total + coef[x0 + x, tap, pl.ds(z, 1), :] * held[k + tap]
                        short = total.astype(BF16)
                        blank = jnp.zeros_like(short)
                        parts[k0 + k, x, h] = jnp.concatenate([blank, short] if x else [short, blank], axis=1)
            for k in (k0, k0 + 1):
                z = group * GROUP + k
                rhs = jnp.concatenate([parts[k, x, h] for x in range(2) for h in range(2)], axis=0)
                both = lax.dot_general(
                    lhs[iy[x0, z] * TABLES + iy[x0 + 1, z]],
                    jnp.concatenate([rhs, rhs], axis=1),
                    (((1,), (1,)), ((), ())),
                    preferred_element_type=F32,
                )
                done[z, :, pl.ds(x0 * rows, 2 * rows)] = both.astype(BF16)
        result(step).start()

    pltpu.make_async_copy(done, out, outs).wait()


def smooth_zy(jacobian, smooth_y, smooth_z, index_y, index_z):
    rows, slab, ny, nz = jacobian.shape
    return pl.pallas_call(
        zy_kernel,
        out_shape=jax.ShapeDtypeStruct((nz, ny, slab * rows), BF16),
        in_specs=[HBM] * 5,
        out_specs=HBM,
        scratch_shapes=[
            pltpu.VMEM((slab, nz + 2 * BAND, rows, ny), F32),
            pltpu.VMEM((slab, TAPS, nz, ny), F32),
            pltpu.VMEM((TABLES * TABLES, ny, 4 * ny), BF16),
            pltpu.VMEM((nz, ny, slab * rows), BF16),
            pltpu.VMEM(smooth_y.shape, F32),
            pltpu.VMEM(smooth_z.shape, F32),
            pltpu.SMEM(index_y.shape, jnp.int32),
            pltpu.VMEM(index_z.shape, jnp.int32),
            pltpu.SemaphoreType.DMA((slab // 2 * nz // GROUP,)),
            pltpu.SemaphoreType.DMA,
            pltpu.SemaphoreType.DMA((4,)),
        ],
        compiler_params=pltpu.CompilerParams(vmem_limit_bytes=60 * 2**20),
        name="smooth_zy",
    )(jnp.swapaxes(jacobian, 2, 3), smooth_y, smooth_z, index_y, index_z)


def coef_kernel(place, index_x, table_x, out, bands):
    z, y0 = place[0], place[1]
    nx = table_x.shape[1]
    _, columns, lanes = out.shape
    for t in range(TABLES):
        for tap in range(TAPS):
            bands[t, tap] = jnp.broadcast_to(band_column(table_x[t], tap), (nx, lanes))
    row = index_x[pl.ds(z, 1), :]
    sub = lax.broadcasted_iota(jnp.int32, (columns, row.shape[1]), 0)
    lan = lax.broadcasted_iota(jnp.int32, (columns, row.shape[1]), 1)
    label = jnp.sum(jnp.where(lan == sub + y0, row, 0).astype(F32), axis=1, keepdims=True)
    label = jnp.broadcast_to(label, (columns, lanes))

    lane = lax.broadcasted_iota(jnp.int32, label.shape, 1)

    @pl.loop(0, out.shape[0])
    def _(cell):
        total = jnp.zeros(label.shape, F32)
        for k in range(4):
            for tap in range(TAPS):
                row = pl.ds(cell * 4 + k, 1)
                picked = jnp.broadcast_to(bands[0, tap, row, :], label.shape)
                for t in range(1, TABLES):
                    picked = jnp.where(label == t, bands[t, tap, row, :], picked)
                total = jnp.where(lane == k * TAPS + tap, picked, total)
        out[cell] = total


def x_coefs(place, index_x, smooth_x):
    nx = smooth_x.shape[1]
    return pl.pallas_call(
        coef_kernel,
        out_shape=jax.ShapeDtypeStruct((nx // 4, 16, 128), F32),
        in_specs=[SMEM, VMEM, VMEM],
        out_specs=VMEM,
        scratch_shapes=[pltpu.VMEM((TABLES, TAPS, nx, 128), F32)],
        compiler_params=pltpu.CompilerParams(vmem_limit_bytes=12 * 2**20),
        cost_estimate=pl.CostEstimate(flops=4 * 2**20, bytes_accessed=4 * 2**20, transcendentals=0),
        name="x_coefs",
    )(place, jnp.swapaxes(index_x, 0, 1), smooth_x)


def x_kernel(part, coef, got, out, wide):
    nx, columns, lanes = out.shape
    cells = nx // 4
    left = lax.broadcasted_iota(jnp.int32, (columns, 128), 1) < 64
    for edge in range(4):
        wide[edge + part * (nx + 4)] = jnp.zeros(wide.shape[1:], F32)

    for k in range(1 - part, cells + 2 - part):
        cell = part * cells + k - 1
        for parity in range(2):
            for zh in range(2):
                first = zh * 64 + cell // 4 * 16 + parity * 4 + cell % 4
                use = pl.ds((parity * 2 + zh) * 128, 128)
                for pair in range(2):
                    a = got[first, :, pl.ds(pair * 128, 128)].astype(F32)
                    b = got[first + 8, :, pl.ds(pair * 128, 128)].astype(F32)
                    base = k * 4 + pair * 2
                    wide[base, :, use] = jnp.where(left, a, pltpu.roll(b, 64, 1))
                    wide[base + 1, :, use] = jnp.where(left, pltpu.roll(a, 64, 1), b)

    for x in range(nx):
        taps = coef[part * cells + x // 4]
        totals = [None] * (lanes // 128)
        for tap in range(TAPS):
            column = x % 4 * TAPS + tap
            factor = jnp.broadcast_to(taps[:, column : column + 1], (columns, 128))
            for block in range(lanes // 128):
                term = factor * wide[x + tap + 4 - BAND, :, pl.ds(block * 128, 128)]
                totals[block] = term if tap == 0 else totals[block] + term
        for block in range(lanes // 128):
            out[x, :, pl.ds(block * 128, 128)] = totals[block].astype(BF16)


def smooth_x_local(part, coef, got):
    nx, columns = coef.shape[0] * 2, coef.shape[1]
    return pl.pallas_call(
        functools.partial(x_kernel, part),
        out_shape=jax.ShapeDtypeStruct((nx, columns, 512), BF16),
        in_specs=[VMEM, VMEM],
        out_specs=VMEM,
        scratch_shapes=[pltpu.VMEM((nx + 8, columns, 512), F32)],
        compiler_params=pltpu.CompilerParams(vmem_limit_bytes=12 * 2**20),
        name="smooth_x",
    )(coef, got).reshape(nx * columns, 512)


def add_up(parts):
    while len(parts) > 1:
        parts = [a + b for a, b in zip(parts[::2], parts[1::2])] + parts[len(parts) // 2 * 2 :]
    return parts[0]


def gram_kernel(core, own_a, own_b, right_a, right_b, *rest):
    out = rest[-1]
    which = core[0]
    for part in range(2):
        piece = sum(
            lax.dot_general(
                own[...],
                right[:, part * 256 : (part + 1) * 256],
                (((0,), (0,)), ((), ())),
                preferred_element_type=F32,
            )
            for own, right in ((own_a, right_a), (own_b, right_b))
        ).astype(BF16)
        for x in range(4):
            for zh in range(2):
                start = ((x % 2 * 2 + zh) * 2 + x // 2) * 64
                out[x, part * 2 + which, pl.ds(zh * 64, 64), :] = piece[start : start + 64]


def gram(core, own, right, *held):
    return pl.pallas_call(
        gram_kernel,
        out_shape=jax.ShapeDtypeStruct((4, 4, 128, 256), BF16),
        in_specs=[SMEM] + [VMEM] * (4 + len(held)),
        out_specs=VMEM,
        input_output_aliases={5: 0} if held else {},
        compiler_params=pltpu.CompilerParams(vmem_limit_bytes=16 * 2**20),
        cost_estimate=pl.CostEstimate(flops=2**29, bytes_accessed=2**21, transcendentals=0),
        name="gram",
    )(core, *own, *right, *held)


def sum_plane_kernel(got, out):
    for zh in range(2):
        for pair in range(2):
            rows, lanes = pl.ds(zh * 64, 64), pl.ds(pair * 128, 128)
            total = add_up([got[k, rows, lanes].astype(F32) for k in range(got.shape[0])])
            left = lax.broadcasted_iota(jnp.int32, (32, 128), 1) < 64
            upper, lower = total[:32], total[32:]
            out[zh * 4 + pair * 2] = jnp.where(left, upper, pltpu.roll(lower, 64, 1))
            out[zh * 4 + pair * 2 + 1] = jnp.where(left, pltpu.roll(upper, 64, 1), lower)


def sum_plane(got):
    return pl.pallas_call(
        sum_plane_kernel,
        out_shape=jax.ShapeDtypeStruct((8, 32, 128), F32),
        in_specs=[VMEM],
        out_specs=VMEM,
        compiler_params=pltpu.CompilerParams(vmem_limit_bytes=8 * 2**20),
        name="sum_plane",
    )(got)


def sum_line_kernel(got, out):
    total = add_up([got[k] for k in range(got.shape[0])])
    out[pl.ds(0, 32), :] = total[:, :64]
    out[pl.ds(32, 32), :] = total[:, 64:]


def sum_line(got):
    return pl.pallas_call(
        sum_line_kernel,
        out_shape=jax.ShapeDtypeStruct((64, 64), F32),
        in_specs=[VMEM],
        out_specs=VMEM,
        compiler_params=pltpu.CompilerParams(vmem_limit_bytes=4 * 2**20),
        name="sum_line",
    )(got)


def body(jacobian, smooth_x, smooth_y, smooth_z, index_x, index_y, index_z):
    sent = smooth_zy(jacobian, smooth_y, smooth_z, index_y, index_z)
    nz, ny, width = sent.shape
    place = jnp.stack([lax.axis_index(("zh", "zl", "x")), lax.axis_index("y") * 16]).astype(jnp.int32)
    coef = x_coefs(place, index_x, smooth_x)
    got = lax.all_to_all(
        sent.reshape(128, nz * ny // 128, width), ("zh", "zl", "x", "y"), 0, 0, tiled=True
    )
    own, other = [], []
    for part in range(2):
        own.append(smooth_x_local(part, coef, got))
        other.append(lax.ppermute(own[part], "core", [(0, 1), (1, 0)]))
    core = lax.axis_index("core").reshape(1).astype(jnp.int32)
    partial = gram(1 - core, own, other, gram(core, own, own))
    plane = lax.all_to_all(partial.reshape(16, 128, 256), ("x", "y"), 0, 0, tiled=True)
    line = lax.all_to_all(sum_plane(plane), ("zh", "zl"), 0, 0, tiled=True)
    return sum_line(line)


def solution(mesh):
    fine = Mesh(mesh.devices.reshape(2, 4, 2, 4, 4), ("zh", "x", "core", "zl", "y"))
    rows, cells = ("zh", "x", "core"), ("zl", "y")
    return jax.shard_map(
        body,
        mesh=fine,
        in_specs=(
            P(rows, cells, None, None),
            P(),
            P(),
            P(),
            P(),
            P(cells, None),
            P(cells, None),
        ),
        out_specs=P(rows, cells),
        check_vma=False,
    )
```

```python
import functools

import jax
import jax.numpy as jnp
from jax import lax
from jax.experimental import pallas as pl
from jax.experimental.pallas import tpu as pltpu
from jax.sharding import Mesh, PartitionSpec as P

BAND = 3
TAPS = 2 * BAND + 1
TABLES = 4
GROUP = 16
AHEAD = 3
F32 = jnp.float32
BF16 = jnp.bfloat16
VMEM = pl.BlockSpec(memory_space=pltpu.VMEM)
SMEM = pl.BlockSpec(memory_space=pltpu.SMEM)
HBM = pl.BlockSpec(memory_space=pltpu.HBM)


def split_table(table):
    high = table.astype(BF16)
    low = (table - high.astype(F32)).astype(BF16)
    return high, low


def band_column(table, tap):
    rows = lax.broadcasted_iota(jnp.int32, table.shape, 0)
    cols = lax.broadcasted_iota(jnp.int32, table.shape, 1)
    return jnp.sum(jnp.where(cols == rows + (tap - BAND), table, 0.0), axis=1, keepdims=True)


def zy_kernel(jac, table_y, table_z, index_y, index_z, out, planes, merged, coef, lhs, done, ty, tz, iy, iz, sems, outs, small):
    slab, _, rows, ny = planes.shape
    pairs = slab // 2
    nz = done.shape[0]
    per = nz // GROUP
    steps = slab // 2 * per
    loads = [
        pltpu.make_async_copy(s, d, small.at[k])
        for k, (s, d) in enumerate(((table_z, tz), (index_z, iz), (table_y, ty), (index_y, iy)))
    ]
    for load in loads:
        load.start()

    def wave(step):
        pair, group = step // per, step % per
        for k in range(GROUP):
            for x in range(2):
                w = group * GROUP + k
                yield pltpu.make_async_copy(
                    jac.at[:, pair * 2 + x, w, :], planes.at[pair * 2 + x, w], sems.at[step]
                )

    def arrived(step):
        pair, group = step // per, step % per
        whole = planes.at[pl.ds(pair * 2, 2), pl.ds(group * GROUP, GROUP)]
        pltpu.make_async_copy(whole, whole, sems.at[step]).wait()
        for w in range(group * GROUP, (group + 1) * GROUP):
            sides = [planes[pair * 2 + x, w] for x in range(2)]
            merged[pair, w + BAND] = jnp.concatenate(sides, axis=1)

    def result(step):
        pair, group = step // per, step % per
        place = (pl.ds(group * GROUP, GROUP), slice(None), pl.ds(pair * 2 * rows, 2 * rows))
        return pltpu.make_async_copy(done.at[place], out.at[place], outs)

    for k, copy in enumerate(wave(0)):
        copy.start(priority=k % 2)
    for pair in range(pairs):
        for edge in range(BAND):
            merged[pair, edge] = jnp.zeros((rows, 2 * ny), F32)
            merged[pair, nz + BAND + edge] = jnp.zeros((rows, 2 * ny), F32)
    loads[0].wait()
    loads[1].wait()
    for tap in range(TAPS):
        cols = [band_column(tz[t], tap) for t in range(TABLES)]
        for pair in range(pairs):
            label = jnp.concatenate([iz[pl.ds(pair * 2 + x, 1), :] for x in range(2)], axis=1)
            picked = jnp.broadcast_to(cols[0], (nz, 2 * ny))
            for t in range(1, TABLES):
                picked = jnp.where(label == t, cols[t], picked)
            coef[pair, tap] = picked
    for step in range(1, AHEAD):
        for k, copy in enumerate(wave(step)):
            copy.start(priority=k % 2)
    loads[2].wait()
    loads[3].wait()
    split = [split_table(ty[t]) for t in range(TABLES)]
    for t in range(TABLES):
        for u in range(TABLES):
            pieces = [split[t][0], split[u][0], split[t][1], split[u][1]]
            lhs[t * TABLES + u] = jnp.concatenate(pieces, axis=1)
    half = rows // 2
    first = lax.broadcasted_iota(jnp.int32, (half, 2 * ny), 1) < ny
    arrived(0)

    for step in range(steps):
        x0, group = step // per * 2, step % per

        if step + AHEAD < steps:
            for k, copy in enumerate(wave(step + AHEAD)):
                copy.start(priority=k % 2)
        parts = {}
        for k0 in range(0, GROUP, 2):
            if k0 + BAND + 1 in (GROUP, GROUP + 1) and step + 1 < steps:
                arrived(step + 1)
            for h in range(2):
                use = pl.ds(h * half, half)
                held = [merged[x0 // 2, group * GROUP + k0 + j, use, :] for j in range(TAPS + 1)]
                for k in range(2):
                    z = group * GROUP + k0 + k
                    total = coef[x0 // 2, 0, pl.ds(z, 1), :] * held[k]
                    for tap in range(1, TAPS):
                        total = total + coef[x0 // 2, tap, pl.ds(z, 1), :] * held[k + tap]
                    for x in range(2):
                        side = jnp.where(first if x == 0 else ~first, total, 0.0)
                        parts[k0 + k, x, h] = side.astype(BF16)
            for k in (k0, k0 + 1):
                z = group * GROUP + k
                rhs = jnp.concatenate([parts[k, x, h] for x in range(2) for h in range(2)], axis=0)
                both = lax.dot_general(
                    lhs[iy[x0, z] * TABLES + iy[x0 + 1, z]],
                    jnp.concatenate([rhs, rhs], axis=1),
                    (((1,), (1,)), ((), ())),
                    preferred_element_type=F32,
                )
                done[z, :, pl.ds(x0 * rows, 2 * rows)] = both.astype(BF16)
        result(step).start()

    pltpu.make_async_copy(done, out, outs).wait()


def smooth_zy(jacobian, smooth_y, smooth_z, index_y, index_z):
    rows, slab, ny, nz = jacobian.shape
    return pl.pallas_call(
        zy_kernel,
        out_shape=jax.ShapeDtypeStruct((nz, ny, slab * rows), BF16),
        in_specs=[HBM] * 5,
        out_specs=HBM,
        scratch_shapes=[
            pltpu.VMEM((slab, nz, rows, ny), F32),
            pltpu.VMEM((slab // 2, nz + 2 * BAND, rows, 2 * ny), F32),
            pltpu.VMEM((slab // 2, TAPS, nz, 2 * ny), F32),
            pltpu.VMEM((TABLES * TABLES, ny, 4 * ny), BF16),
            pltpu.VMEM((nz, ny, slab * rows), BF16),
            pltpu.VMEM(smooth_y.shape, F32),
            pltpu.VMEM(smooth_z.shape, F32),
            pltpu.SMEM(index_y.shape, jnp.int32),
            pltpu.VMEM(index_z.shape, jnp.int32),
            pltpu.SemaphoreType.DMA((slab // 2 * nz // GROUP,)),
            pltpu.SemaphoreType.DMA,
            pltpu.SemaphoreType.DMA((4,)),
        ],
        compiler_params=pltpu.CompilerParams(vmem_limit_bytes=60 * 2**20),
        name="smooth_zy",
    )(jnp.swapaxes(jacobian, 2, 3), smooth_y, smooth_z, index_y, index_z)


def coef_kernel(place, index_x, table_x, out, bands):
    z, y0 = place[0], place[1]
    nx = table_x.shape[1]
    _, columns, lanes = out.shape
    for t in range(TABLES):
        for tap in range(TAPS):
            bands[t, tap] = jnp.broadcast_to(band_column(table_x[t], tap), (nx, lanes))
    row = index_x[pl.ds(z, 1), :]
    sub = lax.broadcasted_iota(jnp.int32, (columns, row.shape[1]), 0)
    lan = lax.broadcasted_iota(jnp.int32, (columns, row.shape[1]), 1)
    label = jnp.sum(jnp.where(lan == sub + y0, row, 0).astype(F32), axis=1, keepdims=True)
    label = jnp.broadcast_to(label, (columns, lanes))

    lane = lax.broadcasted_iota(jnp.int32, label.shape, 1)

    @pl.loop(0, out.shape[0])
    def _(cell):
        total = jnp.zeros(label.shape, F32)
        for k in range(4):
            for tap in range(TAPS):
                row = pl.ds(cell * 4 + k, 1)
                picked = jnp.broadcast_to(bands[0, tap, row, :], label.shape)
                for t in range(1, TABLES):
                    picked = jnp.where(label == t, bands[t, tap, row, :], picked)
                total = jnp.where(lane == k * TAPS + tap, picked, total)
        out[cell] = total


def x_coefs(place, index_x, smooth_x):
    nx = smooth_x.shape[1]
    return pl.pallas_call(
        coef_kernel,
        out_shape=jax.ShapeDtypeStruct((nx // 4, 16, 128), F32),
        in_specs=[SMEM, VMEM, VMEM],
        out_specs=VMEM,
        scratch_shapes=[pltpu.VMEM((TABLES, TAPS, nx, 128), F32)],
        compiler_params=pltpu.CompilerParams(vmem_limit_bytes=12 * 2**20),
        cost_estimate=pl.CostEstimate(flops=4 * 2**20, bytes_accessed=4 * 2**20, transcendentals=0),
        name="x_coefs",
    )(place, jnp.swapaxes(index_x, 0, 1), smooth_x)


def x_kernel(part, coef, got, out, wide):
    nx, columns, lanes = out.shape
    cells = nx // 4
    left = lax.broadcasted_iota(jnp.int32, (columns, 128), 1) < 64
    for edge in range(4):
        wide[edge + part * (nx + 4)] = jnp.zeros(wide.shape[1:], F32)

    for k in range(1 - part, cells + 2 - part):
        cell = part * cells + k - 1
        for parity in range(2):
            for zh in range(2):
                first = zh * 64 + cell // 4 * 16 + parity * 4 + cell % 4
                use = pl.ds((parity * 2 + zh) * 128, 128)
                for pair in range(2):
                    a = got[first, :, pl.ds(pair * 128, 128)].astype(F32)
                    b = got[first + 8, :, pl.ds(pair * 128, 128)].astype(F32)
                    base = k * 4 + pair * 2
                    wide[base, :, use] = jnp.where(left, a, pltpu.roll(b, 64, 1))
                    wide[base + 1, :, use] = jnp.where(left, pltpu.roll(a, 64, 1), b)

    for x in range(nx):
        taps = coef[part * cells + x // 4]
        totals = [None] * (lanes // 128)
        for tap in range(TAPS):
            column = x % 4 * TAPS + tap
            factor = jnp.broadcast_to(taps[:, column : column + 1], (columns, 128))
            for block in range(lanes // 128):
                term = factor * wide[x + tap + 4 - BAND, :, pl.ds(block * 128, 128)]
                totals[block] = term if tap == 0 else totals[block] + term
        for block in range(lanes // 128):
            out[x, :, pl.ds(block * 128, 128)] = totals[block].astype(BF16)


def smooth_x_local(part, coef, got):
    nx, columns = coef.shape[0] * 2, coef.shape[1]
    return pl.pallas_call(
        functools.partial(x_kernel, part),
        out_shape=jax.ShapeDtypeStruct((nx, columns, 512), BF16),
        in_specs=[VMEM, VMEM],
        out_specs=VMEM,
        scratch_shapes=[pltpu.VMEM((nx + 8, columns, 512), F32)],
        compiler_params=pltpu.CompilerParams(vmem_limit_bytes=12 * 2**20),
        name="smooth_x",
    )(coef, got).reshape(nx * columns, 512)


def add_up(parts):
    while len(parts) > 1:
        parts = [a + b for a, b in zip(parts[::2], parts[1::2])] + parts[len(parts) // 2 * 2 :]
    return parts[0]


def gram_kernel(core, own_a, own_b, right_a, right_b, *rest):
    out = rest[-1]
    which = core[0]
    for part in range(2):
        piece = sum(
            lax.dot_general(
                own[...],
                right[:, part * 256 : (part + 1) * 256],
                (((0,), (0,)), ((), ())),
                preferred_element_type=F32,
            )
            for own, right in ((own_a, right_a), (own_b, right_b))
        ).astype(BF16)
        for x in range(4):
            for zh in range(2):
                start = ((x % 2 * 2 + zh) * 2 + x // 2) * 64
                out[x, part * 2 + which, pl.ds(zh * 64, 64), :] = piece[start : start + 64]


def gram(core, own, right, *held):
    return pl.pallas_call(
        gram_kernel,
        out_shape=jax.ShapeDtypeStruct((4, 4, 128, 256), BF16),
        in_specs=[SMEM] + [VMEM] * (4 + len(held)),
        out_specs=VMEM,
        input_output_aliases={5: 0} if held else {},
        compiler_params=pltpu.CompilerParams(vmem_limit_bytes=16 * 2**20),
        cost_estimate=pl.CostEstimate(flops=2**29, bytes_accessed=2**21, transcendentals=0),
        name="gram",
    )(core, *own, *right, *held)


def sum_plane_kernel(got, out):
    for zh in range(2):
        for pair in range(2):
            rows, lanes = pl.ds(zh * 64, 64), pl.ds(pair * 128, 128)
            total = add_up([got[k, rows, lanes].astype(F32) for k in range(got.shape[0])])
            left = lax.broadcasted_iota(jnp.int32, (32, 128), 1) < 64
            upper, lower = total[:32], total[32:]
            out[zh * 4 + pair * 2] = jnp.where(left, upper, pltpu.roll(lower, 64, 1))
            out[zh * 4 + pair * 2 + 1] = jnp.where(left, pltpu.roll(upper, 64, 1), lower)


def sum_plane(got):
    return pl.pallas_call(
        sum_plane_kernel,
        out_shape=jax.ShapeDtypeStruct((8, 32, 128), F32),
        in_specs=[VMEM],
        out_specs=VMEM,
        compiler_params=pltpu.CompilerParams(vmem_limit_bytes=8 * 2**20),
        name="sum_plane",
    )(got)


def sum_line_kernel(got, out):
    total = add_up([got[k] for k in range(got.shape[0])])
    out[pl.ds(0, 32), :] = total[:, :64]
    out[pl.ds(32, 32), :] = total[:, 64:]


def sum_line(got):
    return pl.pallas_call(
        sum_line_kernel,
        out_shape=jax.ShapeDtypeStruct((64, 64), F32),
        in_specs=[VMEM],
        out_specs=VMEM,
        compiler_params=pltpu.CompilerParams(vmem_limit_bytes=4 * 2**20),
        name="sum_line",
    )(got)


def body(jacobian, smooth_x, smooth_y, smooth_z, index_x, index_y, index_z):
    sent = smooth_zy(jacobian, smooth_y, smooth_z, index_y, index_z)
    nz, ny, width = sent.shape
    place = jnp.stack([lax.axis_index(("zh", "zl", "x")), lax.axis_index("y") * 16]).astype(jnp.int32)
    coef = x_coefs(place, index_x, smooth_x)
    got = lax.all_to_all(
        sent.reshape(128, nz * ny // 128, width), ("zh", "zl", "x", "y"), 0, 0, tiled=True
    )
    own, other = [], []
    for part in range(2):
        own.append(smooth_x_local(part, coef, got))
        other.append(lax.ppermute(own[part], "core", [(0, 1), (1, 0)]))
    core = lax.axis_index("core").reshape(1).astype(jnp.int32)
    partial = gram(1 - core, own, other, gram(core, own, own))
    plane = lax.all_to_all(partial.reshape(16, 128, 256), ("x", "y"), 0, 0, tiled=True)
    line = lax.all_to_all(sum_plane(plane), ("zh", "zl"), 0, 0, tiled=True)
    return sum_line(line)


def solution(mesh):
    fine = Mesh(mesh.devices.reshape(2, 4, 2, 4, 4), ("zh", "x", "core", "zl", "y"))
    rows, cells = ("zh", "x", "core"), ("zl", "y")
    return jax.shard_map(
        body,
        mesh=fine,
        in_specs=(
            P(rows, cells, None, None),
            P(),
            P(),
            P(),
            P(),
            P(cells, None),
            P(cells, None),
        ),
        out_specs=P(rows, cells),
        check_vma=False,
    )
```

```python
import functools

import jax
import jax.numpy as jnp
from jax import lax
from jax.experimental import pallas as pl
from jax.experimental.pallas import tpu as pltpu
from jax.sharding import Mesh, PartitionSpec as P

BAND = 3
TAPS = 2 * BAND + 1
TABLES = 4
GROUP = 16
AHEAD = 3
F32 = jnp.float32
BF16 = jnp.bfloat16
VMEM = pl.BlockSpec(memory_space=pltpu.VMEM)
SMEM = pl.BlockSpec(memory_space=pltpu.SMEM)
HBM = pl.BlockSpec(memory_space=pltpu.HBM)


def split_table(table):
    high = table.astype(BF16)
    low = (table - high.astype(F32)).astype(BF16)
    return high, low


def band_column(table, tap):
    rows = lax.broadcasted_iota(jnp.int32, table.shape, 0)
    cols = lax.broadcasted_iota(jnp.int32, table.shape, 1)
    return jnp.sum(jnp.where(cols == rows + (tap - BAND), table, 0.0), axis=1, keepdims=True)


def zy_kernel(jac, table_y, table_z, index_y, index_z, out, planes, merged, coef, lhs, done, ty, tz, iy, iz, sems, outs, small):
    slab, _, rows, ny = planes.shape
    pairs = slab // 2
    nz = done.shape[0]
    per = nz // GROUP
    steps = slab // 2 * per
    loads = [
        pltpu.make_async_copy(s, d, small.at[k])
        for k, (s, d) in enumerate(((table_z, tz), (index_z, iz), (table_y, ty), (index_y, iy)))
    ]
    for load in loads:
        load.start()

    def wave(step):
        pair, group = step // per, step % per
        for k in range(GROUP):
            for x in range(2):
                w = group * GROUP + k
                yield pltpu.make_async_copy(
                    jac.at[:, pair * 2 + x, w, :], planes.at[pair * 2 + x, w], sems.at[step]
                )

    def arrived(step):
        pair, group = step // per, step % per
        whole = planes.at[pl.ds(pair * 2, 2), pl.ds(group * GROUP, GROUP)]
        pltpu.make_async_copy(whole, whole, sems.at[step]).wait()
        for w in range(group * GROUP, (group + 1) * GROUP):
            sides = [planes[pair * 2 + x, w] for x in range(2)]
            merged[pair, w + BAND] = jnp.concatenate(sides, axis=1)

    def result(step):
        pair, group = step // per, step % per
        place = (pl.ds(group * GROUP, GROUP), slice(None), pl.ds(pair * 2 * rows, 2 * rows))
        return pltpu.make_async_copy(done.at[place], out.at[place], outs)

    for k, copy in enumerate(wave(0)):
        copy.start(priority=k % 2)
    for pair in range(pairs):
        for edge in range(BAND):
            merged[pair, edge] = jnp.zeros((rows, 2 * ny), F32)
            merged[pair, nz + BAND + edge] = jnp.zeros((rows, 2 * ny), F32)
    loads[0].wait()
    loads[1].wait()
    for tap in range(TAPS):
        cols = [band_column(tz[t], tap) for t in range(TABLES)]
        for pair in range(pairs):
            label = jnp.concatenate([iz[pl.ds(pair * 2 + x, 1), :] for x in range(2)], axis=1)
            picked = jnp.broadcast_to(cols[0], (nz, 2 * ny))
            for t in range(1, TABLES):
                picked = jnp.where(label == t, cols[t], picked)
            coef[pair, tap] = picked
    for step in range(1, AHEAD):
        for k, copy in enumerate(wave(step)):
            copy.start(priority=k % 2)
    loads[2].wait()
    loads[3].wait()
    split = [split_table(ty[t]) for t in range(TABLES)]
    for t in range(TABLES):
        for u in range(TABLES):
            pieces = [split[t][0], split[u][0], split[t][1], split[u][1]]
            lhs[t * TABLES + u] = jnp.concatenate(pieces, axis=1)
    half = rows // 2
    first = lax.broadcasted_iota(jnp.int32, (half, 2 * ny), 1) < ny
    arrived(0)

    for step in range(steps):
        x0, group = step // per * 2, step % per

        if step + AHEAD < steps:
            for k, copy in enumerate(wave(step + AHEAD)):
                copy.start(priority=k % 2)
        parts = {}
        for k0 in range(0, GROUP, 2):
            if k0 + BAND + 1 in (GROUP, GROUP + 1) and step + 1 < steps:
                arrived(step + 1)
            for h in range(2):
                use = pl.ds(h * half, half)
                held = [merged[x0 // 2, group * GROUP + k0 + j, use, :] for j in range(TAPS + 1)]
                for k in range(2):
                    z = group * GROUP + k0 + k
                    total = coef[x0 // 2, 0, pl.ds(z, 1), :] * held[k]
                    for tap in range(1, TAPS):
                        total = total + coef[x0 // 2, tap, pl.ds(z, 1), :] * held[k + tap]
                    for x in range(2):
                        side = jnp.where(first if x == 0 else ~first, total, 0.0)
                        parts[k0 + k, x, h] = side.astype(BF16)
            for k in (k0, k0 + 1):
                z = group * GROUP + k
                rhs = jnp.concatenate([parts[k, x, h] for x in range(2) for h in range(2)], axis=0)
                both = lax.dot_general(
                    lhs[iy[x0, z] * TABLES + iy[x0 + 1, z]],
                    jnp.concatenate([rhs, rhs], axis=1),
                    (((1,), (1,)), ((), ())),
                    preferred_element_type=F32,
                )
                done[z, :, pl.ds(x0 * rows, 2 * rows)] = both.astype(BF16)
        result(step).start()

    pltpu.make_async_copy(done, out, outs).wait()


def smooth_zy(jacobian, smooth_y, smooth_z, index_y, index_z):
    rows, slab, ny, nz = jacobian.shape
    return pl.pallas_call(
        zy_kernel,
        out_shape=jax.ShapeDtypeStruct((nz, ny, slab * rows), BF16),
        in_specs=[HBM] * 5,
        out_specs=HBM,
        scratch_shapes=[
            pltpu.VMEM((slab, nz, rows, ny), F32),
            pltpu.VMEM((slab // 2, nz + 2 * BAND, rows, 2 * ny), F32),
            pltpu.VMEM((slab // 2, TAPS, nz, 2 * ny), F32),
            pltpu.VMEM((TABLES * TABLES, ny, 4 * ny), BF16),
            pltpu.VMEM((nz, ny, slab * rows), BF16),
            pltpu.VMEM(smooth_y.shape, F32),
            pltpu.VMEM(smooth_z.shape, F32),
            pltpu.SMEM(index_y.shape, jnp.int32),
            pltpu.VMEM(index_z.shape, jnp.int32),
            pltpu.SemaphoreType.DMA((slab // 2 * nz // GROUP,)),
            pltpu.SemaphoreType.DMA,
            pltpu.SemaphoreType.DMA((4,)),
        ],
        compiler_params=pltpu.CompilerParams(vmem_limit_bytes=60 * 2**20),
        name="smooth_zy",
    )(jnp.swapaxes(jacobian, 2, 3), smooth_y, smooth_z, index_y, index_z)


def coef_kernel(place, index_x, table_x, out, bands):
    z, y0 = place[0], place[1]
    nx = table_x.shape[1]
    _, columns, lanes = out.shape
    for t in range(TABLES):
        for tap in range(TAPS):
            bands[t, tap] = jnp.broadcast_to(band_column(table_x[t], tap), (nx, lanes))
    row = index_x[pl.ds(z, 1), :]
    sub = lax.broadcasted_iota(jnp.int32, (columns, row.shape[1]), 0)
    lan = lax.broadcasted_iota(jnp.int32, (columns, row.shape[1]), 1)
    label = jnp.sum(jnp.where(lan == sub + y0, row, 0).astype(F32), axis=1, keepdims=True)
    label = jnp.broadcast_to(label, (columns, lanes))

    lane = lax.broadcasted_iota(jnp.int32, label.shape, 1)

    @pl.loop(0, out.shape[0])
    def _(cell):
        total = jnp.zeros(label.shape, F32)
        for k in range(4):
            for tap in range(TAPS):
                row = pl.ds(cell * 4 + k, 1)
                picked = jnp.broadcast_to(bands[0, tap, row, :], label.shape)
                for t in range(1, TABLES):
                    picked = jnp.where(label == t, bands[t, tap, row, :], picked)
                total = jnp.where(lane == k * TAPS + tap, picked, total)
        out[cell] = total


def x_coefs(place, index_x, smooth_x):
    nx = smooth_x.shape[1]
    return pl.pallas_call(
        coef_kernel,
        out_shape=jax.ShapeDtypeStruct((nx // 4, 16, 128), F32),
        in_specs=[SMEM, VMEM, VMEM],
        out_specs=VMEM,
        scratch_shapes=[pltpu.VMEM((TABLES, TAPS, nx, 128), F32)],
        compiler_params=pltpu.CompilerParams(vmem_limit_bytes=12 * 2**20),
        cost_estimate=pl.CostEstimate(flops=4 * 2**20, bytes_accessed=4 * 2**20, transcendentals=0),
        name="x_coefs",
    )(place, jnp.swapaxes(index_x, 0, 1), smooth_x)


def x_kernel(start, coef, got, out, wide):
    nx, columns, lanes = out.shape
    count = nx // 4
    left = lax.broadcasted_iota(jnp.int32, (columns, 128), 1) < 64

    for k in range(count + 2):
        cell = start + k - 1
        if not 0 <= cell < coef.shape[0]:
            for x in range(4):
                wide[k * 4 + x] = jnp.zeros(wide.shape[1:], F32)
            continue
        for parity in range(2):
            for zh in range(2):
                first = zh * 64 + cell // 4 * 16 + parity * 4 + cell % 4
                use = pl.ds((parity * 2 + zh) * 128, 128)
                for pair in range(2):
                    a = got[first, :, pl.ds(pair * 128, 128)].astype(F32)
                    b = got[first + 8, :, pl.ds(pair * 128, 128)].astype(F32)
                    base = k * 4 + pair * 2
                    wide[base, :, use] = jnp.where(left, a, pltpu.roll(b, 64, 1))
                    wide[base + 1, :, use] = jnp.where(left, pltpu.roll(a, 64, 1), b)

    for x in range(nx):
        taps = coef[start + x // 4]
        totals = [None] * (lanes // 128)
        for tap in range(TAPS):
            column = x % 4 * TAPS + tap
            factor = jnp.broadcast_to(taps[:, column : column + 1], (columns, 128))
            for block in range(lanes // 128):
                term = factor * wide[x + tap + 4 - BAND, :, pl.ds(block * 128, 128)]
                totals[block] = term if tap == 0 else totals[block] + term
        for block in range(lanes // 128):
            out[x, :, pl.ds(block * 128, 128)] = totals[block].astype(BF16)


def smooth_x_local(start, count, coef, got):
    nx, columns = count * 4, coef.shape[1]
    return pl.pallas_call(
        functools.partial(x_kernel, start),
        out_shape=jax.ShapeDtypeStruct((nx, columns, 512), BF16),
        in_specs=[VMEM, VMEM],
        out_specs=VMEM,
        scratch_shapes=[pltpu.VMEM((nx + 8, columns, 512), F32)],
        compiler_params=pltpu.CompilerParams(vmem_limit_bytes=12 * 2**20),
        name="smooth_x",
    )(coef, got).reshape(nx * columns, 512)


def add_up(parts):
    while len(parts) > 1:
        parts = [a + b for a, b in zip(parts[::2], parts[1::2])] + parts[len(parts) // 2 * 2 :]
    return parts[0]


def product(lefts, rights, lanes):
    return sum(
        lax.dot_general(
            left[...], right[:, lanes], (((0,), (0,)), ((), ())), preferred_element_type=F32
        )
        for left, right in zip(lefts, rights)
    )


def place_piece(out, part, which, piece):
    piece = piece.astype(BF16)
    for x in range(4):
        for zh in range(2):
            start = ((x % 2 * 2 + zh) * 2 + x // 2) * 64
            out[x, part * 2 + which, pl.ds(zh * 64, 64), :] = piece[start : start + 64]


def own_kernel(core, *refs):
    *own, out = refs
    for part in range(2):
        place_piece(out, part, core[0], product(own, own, slice(part * 256, (part + 1) * 256)))


def early_kernel(left, right, out):
    for part in range(2):
        lanes = slice(part * 256, (part + 1) * 256)
        out[:, lanes] = product((left,), (right,), lanes)


def late_kernel(core, left, right, early, held, out):
    for part in range(2):
        lanes = slice(part * 256, (part + 1) * 256)
        place_piece(out, part, core[0], early[:, lanes] + product((left,), (right,), lanes))


def gram(kernel, shape, operands, aliases):
    first = [SMEM] if operands[0].ndim == 1 else [VMEM]
    return pl.pallas_call(
        kernel,
        out_shape=shape,
        in_specs=first + [VMEM] * (len(operands) - 1),
        out_specs=VMEM,
        input_output_aliases=aliases,
        compiler_params=pltpu.CompilerParams(vmem_limit_bytes=16 * 2**20),
        cost_estimate=pl.CostEstimate(flops=2**29, bytes_accessed=2**21, transcendentals=0),
        name="gram",
    )(*operands)


def sum_plane_kernel(got, out):
    for zh in range(2):
        for pair in range(2):
            rows, lanes = pl.ds(zh * 64, 64), pl.ds(pair * 128, 128)
            total = add_up([got[k, rows, lanes].astype(F32) for k in range(got.shape[0])])
            left = lax.broadcasted_iota(jnp.int32, (32, 128), 1) < 64
            upper, lower = total[:32], total[32:]
            out[zh * 4 + pair * 2] = jnp.where(left, upper, pltpu.roll(lower, 64, 1))
            out[zh * 4 + pair * 2 + 1] = jnp.where(left, pltpu.roll(upper, 64, 1), lower)


def sum_plane(got):
    return pl.pallas_call(
        sum_plane_kernel,
        out_shape=jax.ShapeDtypeStruct((8, 32, 128), F32),
        in_specs=[VMEM],
        out_specs=VMEM,
        compiler_params=pltpu.CompilerParams(vmem_limit_bytes=8 * 2**20),
        name="sum_plane",
    )(got)


def sum_line_kernel(got, out):
    total = add_up([got[k] for k in range(got.shape[0])])
    out[pl.ds(0, 32), :] = total[:, :64]
    out[pl.ds(32, 32), :] = total[:, 64:]


def sum_line(got):
    return pl.pallas_call(
        sum_line_kernel,
        out_shape=jax.ShapeDtypeStruct((64, 64), F32),
        in_specs=[VMEM],
        out_specs=VMEM,
        compiler_params=pltpu.CompilerParams(vmem_limit_bytes=4 * 2**20),
        name="sum_line",
    )(got)


def body(jacobian, smooth_x, smooth_y, smooth_z, index_x, index_y, index_z):
    sent = smooth_zy(jacobian, smooth_y, smooth_z, index_y, index_z)
    nz, ny, width = sent.shape
    place = jnp.stack([lax.axis_index(("zh", "zl", "x")), lax.axis_index("y") * 16]).astype(jnp.int32)
    coef = x_coefs(place, index_x, smooth_x)
    got = lax.all_to_all(
        sent.reshape(128, nz * ny // 128, width), ("zh", "zl", "x", "y"), 0, 0, tiled=True
    )
    own, other = [], []
    for start, count in ((0, 8), (8, 8)):
        own.append(smooth_x_local(start, count, coef, got))
        other.append(lax.ppermute(own[-1], "core", [(0, 1), (1, 0)]))
    core = lax.axis_index("core").reshape(1).astype(jnp.int32)
    blocks = jax.ShapeDtypeStruct((4, 4, 128, 256), BF16)
    held = gram(own_kernel, blocks, (core, *own), {})
    early = gram(early_kernel, jax.ShapeDtypeStruct((512, 512), F32), (own[0], other[0]), {})
    partial = gram(late_kernel, blocks, (1 - core, own[1], other[1], early, held), {4: 0})
    plane = lax.all_to_all(partial.reshape(16, 128, 256), ("x", "y"), 0, 0, tiled=True)
    line = lax.all_to_all(sum_plane(plane), ("zh", "zl"), 0, 0, tiled=True)
    return sum_line(line)


def solution(mesh):
    fine = Mesh(mesh.devices.reshape(2, 4, 2, 4, 4), ("zh", "x", "core", "zl", "y"))
    rows, cells = ("zh", "x", "core"), ("zl", "y")
    return jax.shard_map(
        body,
        mesh=fine,
        in_specs=(
            P(rows, cells, None, None),
            P(),
            P(),
            P(),
            P(),
            P(cells, None),
            P(cells, None),
        ),
        out_specs=P(rows, cells),
        check_vma=False,
    )
```
